32 devices in a mesh: groups: 1, gx: 4 (over y, x), yz: 8 (over z, core).
Axes of the slice: x: 2, y: 2, z: 4, core: 2. Of those that a mesh axis runs over, the one named last changes fastest.
Arguments:
- hidden_in: bfloat16 [128, 8192], P(('groups', 'gx'), 'yz'), may hold values from -12 to 12
- norm_gain_a: float32 [8192], P('yz'), may hold values from 0.1 to 1.9
- mixer_projection: bfloat16 [2, 16384, 8192], P(None, 'gx', 'yz'), may hold values from -0.0625 to 0.0625
- conv_weight: float32 [4, 16384], P(None, ('gx', 'yz')), may hold values from -3 to 3
- conv_bias: float32 [16384], P(('gx', 'yz')), may hold values from -0.5 to 0.5
- conv_state: bfloat16 [16384, 3, 128], P(('gx', 'yz'), None, 'groups'), may hold values from -6 to 6
- ssm_state: bfloat16 [16384, 16, 128], P(('gx', 'yz'), None, 'groups'), may hold values from -6 to 6
- reset_ids: int32 [16], P('groups'), may hold values from 0 to 127
- x_proj: bfloat16 [16384, 544], P(('gx', 'yz')), may hold values from -0.09375 to 0.09375
- dt_proj: bfloat16 [512, 16384], P(None, ('gx', 'yz')), may hold values from -0.25 to 0.25
- dt_bias: float32 [16384], P(('gx', 'yz')), may hold values from -4 to -1
- a_log: float32 [16, 16384], P(None, ('gx', 'yz')), may hold values from 0 to 3
- d_skip: float32 [16384], P(('gx', 'yz')), may hold values from -1 to 2
- mixer_output: bfloat16 [16384, 8192], P('gx', 'yz'), may hold values from -0.046875 to 0.046875
- norm_gain_b: float32 [8192], P('yz'), may hold values from 0.5 to 1.5
- attention_projection: bfloat16 [8192, 8, 1280], P('yz', 'gx'), may hold values from -0.0625 to 0.0625
- head_output: bfloat16 [8192, 8192], P('gx', 'yz'), may hold values from -0.0625 to 0.0625
- kv_cache: bfloat16 [128, 64, 8, 256], P(('groups', 'yz'), None, 'gx'), as said below
- lengths: int32 [128], P(('groups', 'yz')), may hold values from 1 to 64, 4096 in all
- assign: int32 [128], P('groups'), may hold values from 0 to 127, each once
Outputs:
- hidden_out: bfloat16 [128, 8192], P(('groups', 'gx'), 'yz')
- ssm_new: bfloat16 [16384, 16, 128], P(('gx', 'yz'), None, 'groups')
- conv_new: bfloat16 [16384, 3, 128], P(('gx', 'yz'), None, 'groups')
- fresh_kv: bfloat16 [128, 8, 256], P(('groups', 'yz'), 'gx')
The draws below stay inside these ranges and needn't reach their ends.
Inputs may be any that keep to these rules, and one draw needn't show every extreme that they name: `reset_ids`: ids of admitted requests whose conv and recurrent states start from zero; an id may repeat. `lengths`: at least one slot holds 64 valid positions. `assign`: each request is held by exactly one slot. `kv_cache`: positions at or past a slot's length hold arbitrary values that must not be read.
All inputs are finite; a program needn't handle non-finite values. No bound on the sum of `lengths` on one device may be relied on, other than what follows from the above.
Results may differ from the reference program's by a relative error of at most 0.03.
Values may be sent and summed in bfloat16 or wider, within the bound.
No kernel may reach another device: no remote copies, remote signals or barrier semaphores. Data moves between devices by JAX's collectives and lax.ppermute only.
A program may use at most 128 MiB of HBM per device.

```python
import math
import jax
import jax.numpy as jnp
import numpy as np
from jax import lax

MODEL_WIDTH = 8192
E = 16384
N = 16
KC = 4
R = 512
QUERY_HEADS = 64
KEY_VALUE_HEADS = 8
HEAD_SIZE = 128
SLOT_POSITIONS = 64
REQUEST_TOTAL = 128
RESETS = 16
GROUP_COLUMNS = 1280
N_GX = 4
N_YZ = 8


def draw_hidden_in(key, part):
    key = jax.random.fold_in(key, 5)
    first = jax.random.fold_in(key, 0)
    array_shape = (REQUEST_TOTAL, MODEL_WIDTH)
    ramp = jnp.exp(jnp.log(4.0) * jnp.arange(MODEL_WIDTH, dtype=jnp.float32) / (MODEL_WIDTH - 1))[None, :]
    base = jnp.clip(jax.random.normal(first, array_shape, jnp.float32), -3.0, 3.0)
    return (base * ramp).astype(jnp.bfloat16)


def draw_kv_cache(key, part):
    key = jax.random.fold_in(key, 11)
    first = jax.random.fold_in(key, 0)
    array_shape = (REQUEST_TOTAL, SLOT_POSITIONS, KEY_VALUE_HEADS, 2 * HEAD_SIZE)
    base = jax.random.normal(first, array_shape, jnp.float32)
    return base.astype(jnp.bfloat16)


def place_ends(array, key, smallest, top_value):
    place = [jax.random.randint(jax.random.fold_in(key, axis), (), 0, length) for axis, length in enumerate(array.shape)]
    widest = array.shape.index(max(array.shape))
    next_to = place[:widest] + [(place[widest] + 1) % array.shape[widest]] + place[widest + 1:]
    return array.at[tuple(place)].set(smallest).at[tuple(next_to)].set(top_value)


def shard_levels(key, shape, cuts, least, high):
    def one(axis_at, blocks):
        steps = jax.random.uniform(jax.random.fold_in(jax.random.fold_in(key, 6), axis_at), (blocks,), jnp.float32, least / len(cuts), high / len(cuts))
        return jnp.repeat(jnp.exp(steps), shape[axis_at] // blocks).reshape((-1,) + (1,) * (len(shape) - axis_at - 1))

    level = one(*cuts[0])
    for cut in cuts[1:]:
        level = level * one(*cut)
    return level


def length_profile(count, total, bound, lean):
    portions = [(1 << 20) // math.isqrt(grade ** lean) + 1 for grade in range(2, count + 1)]
    spare, holding = total - bound - (count - 1), [1] * (count - 1)
    while spare > 0:
        candidates = [i for i in range(count - 1) if holding[i] < bound]
        whole, budget = sum([portions[i] for i in candidates]), spare
        for i in candidates:
            addition = min(bound - holding[i], max(1, budget * portions[i] // whole), spare)
            holding[i] = holding[i] + addition
            spare = spare - addition
    return np.array([bound] + holding)


def uneven_parts(key, count, total, reach, lean):
    if count == 2:
        one = jax.random.randint(key, (), max(1, total - reach), min(reach, total - 1) + 1)
        return jnp.stack([one, total - one])
    sizes = jnp.asarray(length_profile(count, total, reach, lean), jnp.int32)
    twos = (count - 1) // 2
    source_of, taker = sizes[1:1 + 2 * twos:2], sizes[2:2 + 2 * twos:2]
    margin = jnp.minimum(source_of - 1, reach - taker)
    moved = jax.random.randint(jax.random.fold_in(key, 1), (twos,), 0, 1 << 20) % (margin + 1)
    sizes = sizes.at[1:1 + 2 * twos:2].set(source_of - moved).at[2:2 + 2 * twos:2].set(taker + moved)
    return sizes[jax.random.permutation(jax.random.fold_in(key, 2), count)]


def centred(stream_key, extent, width, most, pieces=(), kind=jnp.bfloat16):
    drawn = width * jax.random.normal(stream_key, extent, jnp.float32)
    if pieces:
        drawn = drawn * shard_levels(stream_key, extent, pieces, -0.22, 0.18)
    return jnp.clip(drawn, -most, most).astype(kind)


def setup_inputs(seed: int = 0, part: int = 0) -> dict:
    key_list = jax.random.split(jax.random.key(seed), 21)
    own_keys = jax.random.split(jax.random.fold_in(key_list[20], part), 21)
    return {
        "hidden_in": draw_hidden_in(jax.random.fold_in(jax.random.fold_in(key_list[20], part), 71), part),
        "norm_gain_a": jnp.clip(1.0 + 0.18 * jax.random.normal(key_list[1], (MODEL_WIDTH,), jnp.float32), 0.1, 1.9),
        "mixer_projection": centred(key_list[2], (2, E, MODEL_WIDTH), MODEL_WIDTH ** -0.5, 0.0625, ((1, 4), (2, 8))),
        "conv_weight": centred(key_list[3], (KC, E), 0.5, 3.0, ((1, 32),), jnp.float32),
        "conv_bias": jnp.clip(jax.random.uniform(key_list[4], (E,), jnp.float32, -0.5, 0.5) * shard_levels(key_list[4], (E,), ((0, 32),), -0.4, 0.0), -0.5, 0.5),
        "conv_state": centred(own_keys[5], (E, KC - 1, REQUEST_TOTAL), 1.0, 6.0, ((0, 32),)),
        "ssm_state": centred(own_keys[6], (E, N, REQUEST_TOTAL), 1.0, 6.0, ((0, 32),)),
        "reset_ids": place_ends(jax.random.randint(own_keys[7], (RESETS,), 0, REQUEST_TOTAL), jax.random.fold_in(own_keys[7], 1), 0, REQUEST_TOTAL - 1).astype(jnp.int32),
        "x_proj": centred(key_list[8], (E, R + 2 * N), (E // 4) ** -0.5, 0.09375, ((0, 32),)),
        "dt_proj": centred(key_list[9], (R, E), R ** -0.5, 0.25, ((1, 32),)),
        "dt_bias": jnp.clip(-4.0 + 3.0 * jax.random.uniform(key_list[10], (E,), jnp.float32) ** shard_levels(key_list[10], (E,), ((0, 32),), -0.2, 0.2), -4.0, -1.0),
        "a_log": jnp.clip(3.0 * jax.random.uniform(key_list[11], (N, E), jnp.float32) ** shard_levels(key_list[11], (N, E), ((1, 32),), -0.2, 0.2), 0.0, 3.0),
        "d_skip": jnp.clip(-1.0 + 3.0 * jax.random.uniform(key_list[12], (E,), jnp.float32) ** shard_levels(key_list[12], (E,), ((0, 32),), -0.2, 0.2), -1.0, 2.0),
        "mixer_output": centred(key_list[13], (E, MODEL_WIDTH), E ** -0.5, 0.046875, ((0, 4), (1, 8))),
        "norm_gain_b": jnp.clip(1.0 + 0.1 * jax.random.normal(key_list[14], (MODEL_WIDTH,), jnp.float32), 0.5, 1.5),
        "attention_projection": centred(key_list[15], (MODEL_WIDTH, KEY_VALUE_HEADS, GROUP_COLUMNS), MODEL_WIDTH ** -0.5, 0.0625, ((0, 8), (1, 4))),
        "head_output": centred(key_list[16], (QUERY_HEADS * HEAD_SIZE, MODEL_WIDTH), (QUERY_HEADS * HEAD_SIZE) ** -0.5, 0.0625, ((0, 4), (1, 8))),
        "kv_cache": draw_kv_cache(jax.random.fold_in(jax.random.fold_in(key_list[20], part), 71), part),
        "lengths": uneven_parts(own_keys[18], REQUEST_TOTAL, REQUEST_TOTAL * SLOT_POSITIONS // 2, SLOT_POSITIONS, 2).astype(jnp.int32),
        "assign": jax.random.permutation(own_keys[19], REQUEST_TOTAL).astype(jnp.int32),
    }


def norm_rows(values, gain):
    wide = values.astype(jnp.float32)
    scale = lax.rsqrt(lax.optimization_barrier(jnp.mean(wide * wide, axis=1, keepdims=True)) + 1e-05)
    return (wide * scale * gain[None, :]).astype(jnp.bfloat16)

def rounded(value):
    return lax.optimization_barrier(value.astype(jnp.bfloat16)).astype(jnp.float32)

def reference(hidden_in, norm_gain_a, mixer_projection, conv_weight, conv_bias, conv_state, ssm_state, reset_ids, x_proj, dt_proj, dt_bias, a_log, d_skip, mixer_output, norm_gain_b, attention_projection, head_output, kv_cache, lengths, assign):
    hn = norm_rows(hidden_in, norm_gain_a)
    dblock = MODEL_WIDTH // N_YZ
    accum = jnp.zeros((2, E, REQUEST_TOTAL), jnp.float32)
    for block in range(N_YZ):
        feats = hn[:, block * dblock:(block + 1) * dblock].astype(jnp.float32)
        weights = mixer_projection[:, :, block * dblock:(block + 1) * dblock].astype(jnp.float32)
        accum = accum + rounded(jnp.einsum('pcd,bd->pcb', weights, feats))
    xz = accum.astype(jnp.bfloat16)
    xval = xz[0]
    zval = xz[1]
    reset = jnp.any(reset_ids[:, None] == jnp.arange(REQUEST_TOTAL, dtype=jnp.int32)[None, :], axis=0)
    conv_old = jnp.where(reset[None, None, :], jnp.zeros_like(conv_state), conv_state)
    window = jnp.concatenate([conv_old, xval[:, None, :]], axis=1)
    conv_new = window[:, 1:, :]
    mixed_conv = lax.optimization_barrier(jnp.sum(jnp.transpose(conv_weight)[:, :, None] * window.astype(jnp.float32), axis=1)) + conv_bias[:, None]
    xa = jax.nn.silu(mixed_conv).astype(jnp.bfloat16)
    proj = jnp.dot(jnp.transpose(x_proj), xa, preferred_element_type=jnp.float32)
    dt_low = proj[:R].astype(jnp.bfloat16)
    bmat = proj[R:R + N]
    cmat = proj[R + N:]
    dt = jax.nn.softplus(jnp.dot(jnp.transpose(dt_proj), dt_low, preferred_element_type=jnp.float32) + dt_bias[:, None])
    rates = -jnp.exp(jnp.transpose(a_log))
    old = jnp.where(reset[None, None, :], jnp.zeros((), jnp.float32), ssm_state.astype(jnp.float32))
    xa_wide = xa.astype(jnp.float32)
    state = jnp.exp(dt[:, None, :] * rates[:, :, None]) * old + dt[:, None, :] * bmat[None, :, :] * xa_wide[:, None, :]
    ssm_new = state.astype(jnp.bfloat16)
    yval = lax.optimization_barrier(jnp.sum(state * cmat[None, :, :], axis=1)) + d_skip[:, None] * xa_wide
    gated = (yval * jax.nn.silu(zval.astype(jnp.float32))).astype(jnp.bfloat16)
    eblock = E // N_GX
    mamba_sum = hidden_in.astype(jnp.float32)
    for block in range(N_GX):
        part_rows = gated[block * eblock:(block + 1) * eblock]
        mamba_sum = mamba_sum + rounded(jnp.dot(jnp.transpose(part_rows), mixer_output[block * eblock:(block + 1) * eblock], preferred_element_type=jnp.float32))
    h1 = mamba_sum.astype(jnp.bfloat16)
    hm = norm_rows(h1, norm_gain_b)
    flattened = attention_projection.reshape(MODEL_WIDTH, KEY_VALUE_HEADS * GROUP_COLUMNS)
    query_total = jnp.zeros((REQUEST_TOTAL, KEY_VALUE_HEADS * GROUP_COLUMNS), jnp.float32)
    for block in range(N_YZ):
        query_total = query_total + rounded(jnp.dot(hm[:, block * dblock:(block + 1) * dblock], flattened[block * dblock:(block + 1) * dblock], preferred_element_type=jnp.float32))
    query_key_value = query_total.astype(jnp.bfloat16).reshape(REQUEST_TOTAL, KEY_VALUE_HEADS, GROUP_COLUMNS)
    newest_entry = jnp.take(query_key_value, assign, axis=0)
    per_head_group = QUERY_HEADS // KEY_VALUE_HEADS
    fresh_kv = newest_entry[:, :, per_head_group * HEAD_SIZE:]
    query_vector = newest_entry[:, :, :per_head_group * HEAD_SIZE].reshape(REQUEST_TOTAL, KEY_VALUE_HEADS, per_head_group, HEAD_SIZE).astype(jnp.float32)
    key_new = newest_entry[:, :, per_head_group * HEAD_SIZE:(per_head_group + 1) * HEAD_SIZE].astype(jnp.float32)
    value_new = newest_entry[:, :, (per_head_group + 1) * HEAD_SIZE:].astype(jnp.float32)
    keys = kv_cache[..., :HEAD_SIZE].astype(jnp.float32)
    values = kv_cache[..., HEAD_SIZE:].astype(jnp.float32)
    factor = 1.0 / math.sqrt(HEAD_SIZE)
    scores = jnp.einsum('sghd,stgd->sght', query_vector, keys) * factor
    own = jnp.einsum('sghd,sgd->sgh', query_vector, key_new) * factor
    valid = (jnp.arange(SLOT_POSITIONS, dtype=jnp.int32)[None, :] < lengths[:, None])[:, None, None, :]
    top = jnp.maximum(lax.optimization_barrier(jnp.max(jnp.where(valid, scores, -1e+30), axis=-1)), own)
    expo = jnp.where(valid, jnp.exp(scores - top[..., None]), 0.0)
    expo_own = jnp.exp(own - top)
    total = lax.optimization_barrier(jnp.sum(expo, axis=-1)) + expo_own
    weights = (expo / total[..., None]).astype(jnp.bfloat16)
    weight_own = (expo_own / total).astype(jnp.bfloat16)
    attended = jnp.einsum('sght,stgd->sghd', weights.astype(jnp.float32), values) + weight_own.astype(jnp.float32)[..., None] * value_new[:, :, None, :]
    heads = attended.astype(jnp.bfloat16).reshape(REQUEST_TOTAL, QUERY_HEADS * HEAD_SIZE)
    by_request = jnp.take(heads, jnp.argsort(assign), axis=0)
    hblock = QUERY_HEADS * HEAD_SIZE // N_GX
    attn_sum = h1.astype(jnp.float32)
    for block in range(N_GX):
        attn_sum = attn_sum + rounded(jnp.dot(by_request[:, block * hblock:(block + 1) * hblock], head_output[block * hblock:(block + 1) * hblock], preferred_element_type=jnp.float32))
    hidden_out = attn_sum.astype(jnp.bfloat16)
    return (hidden_out, ssm_new, conv_new, fresh_kv)
```

```python
import math

import jax
import jax.numpy as jnp
from jax import lax
from jax.sharding import PartitionSpec as P

F32 = jnp.float32
BF16 = jnp.bfloat16


def swap(value, axis, bits):
    size = lax.axis_size(axis)
    return lax.ppermute(value, axis, [(i, i ^ bits) for i in range(size)])


def pick(stack, index):
    return lax.dynamic_index_in_dim(stack, index, 0, keepdims=False)


def gather_gx(value):
    size = lax.axis_size("gx")
    me = lax.axis_index("gx")
    got = jnp.stack([value] + [swap(value, "gx", k) for k in range(1, size)])
    return jnp.take(got, me ^ jnp.arange(size), axis=0)


def scatter_gx(pieces):
    size = lax.axis_size("gx")
    me = lax.axis_index("gx")
    wire = pieces.astype(BF16)
    got = [swap(pick(wire, me ^ k), "gx", k) for k in range(1, size)]
    total = pick(wire, me).astype(F32)
    for term in got:
        total = total + term.astype(F32)
    return total


def scatter_yz(pieces):
    size = lax.axis_size("yz")
    chips = size // 2
    me = lax.axis_index("yz")
    core, chip = me % 2, me // 2
    pairs = pieces.reshape((chips, 2) + pieces.shape[1:])
    keep = lax.dynamic_index_in_dim(pairs, core, 1, keepdims=False)
    give = lax.dynamic_index_in_dim(pairs, 1 - core, 1, keepdims=False)
    summed = keep.astype(F32) + swap(give.astype(BF16), "yz", 1).astype(F32)
    wire = summed.astype(BF16)
    got = [swap(pick(wire, chip ^ k), "yz", 2 * k) for k in range(1, chips)]
    total = pick(summed, chip)
    for term in got:
        total = total + term.astype(F32)
    return total


def gather_yz(value):
    size = lax.axis_size("yz")
    chips = size // 2
    me = lax.axis_index("yz")
    mine = [value] + [swap(value, "yz", 2 * k) for k in range(1, chips)]
    other = [swap(v, "yz", 1) for v in mine]
    got = jnp.stack([v for pair in zip(mine, other) for v in pair])
    return jnp.take(got, me ^ jnp.arange(size), axis=0)


def sum_all(value):
    rows = value.shape[0]
    core = lax.axis_index("yz") % 2
    halves = value.reshape(2, rows // 2, value.shape[1])
    half = pick(halves, core) + swap(pick(halves, 1 - core).astype(BF16), "yz", 1).astype(F32)
    wire = half.astype(BF16)
    for k in range(1, lax.axis_size("gx")):
        half = half + swap(wire, "gx", k).astype(F32)
    wire = half.astype(BF16)
    for k in range(1, lax.axis_size("yz") // 2):
        half = half + swap(wire, "yz", 2 * k).astype(F32)
    wire = half.astype(BF16)
    other = swap(wire, "yz", 1)
    pair = jnp.stack([wire, other])
    return jnp.concatenate([pick(pair, core), pick(pair, 1 - core)], axis=0).astype(F32)


def on_device(
    hidden_in,
    norm_gain_a,
    mixer_projection,
    conv_weight,
    conv_bias,
    conv_state,
    ssm_state,
    reset_ids,
    x_proj,
    dt_proj,
    dt_bias,
    a_log,
    d_skip,
    mixer_output,
    norm_gain_b,
    attention_projection,
    head_output,
    kv_cache,
    lengths,
    assign,
):
    batch = assign.shape[0]
    yz = lax.axis_size("yz")
    gx = lax.axis_size("gx")
    width = hidden_in.shape[1]
    whole_width = width * yz

    rows_in = gather_gx(hidden_in).reshape(batch, width).astype(F32)
    squares = jnp.sum(rows_in * rows_in, axis=1)
    gained = (rows_in * norm_gain_a[None, :]).astype(BF16)
    channels = mixer_projection.shape[1]
    own = channels // yz

    def project(part):
        return lax.dot_general(
            mixer_projection[part], gained, (((1,), (1,)), ((), ())), preferred_element_type=F32
        ).reshape(yz, own, batch)

    extra = jnp.broadcast_to(squares[None, None, :], (yz, 16, batch))
    xsum = scatter_yz(jnp.concatenate([project(0), extra], axis=1))
    scale = lax.rsqrt(xsum[own] / whole_width + 1e-05)
    xval = (xsum[:own] * scale[None, :]).astype(BF16)
    zval = (scatter_yz(project(1)) * scale[None, :]).astype(BF16)

    reset = jnp.any(reset_ids[:, None] == jnp.arange(batch, dtype=jnp.int32)[None, :], axis=0)
    conv_old = jnp.where(reset[None, None, :], jnp.zeros_like(conv_state), conv_state)
    window = jnp.concatenate([conv_old, xval[:, None, :]], axis=1)
    conv_new = window[:, 1:, :]
    mixed_conv = (
        jnp.sum(jnp.transpose(conv_weight)[:, :, None] * window.astype(F32), axis=1)
        + conv_bias[:, None]
    )
    activated = jax.nn.silu(mixed_conv).astype(BF16)
    proj = sum_all(
        lax.dot_general(
            x_proj, activated, (((0,), (0,)), ((), ())), preferred_element_type=F32
        )
    )
    rank = dt_proj.shape[0]
    nstate = a_log.shape[0]
    dt_low = proj[:rank].astype(BF16)
    bmat = proj[rank : rank + nstate]
    cmat = proj[rank + nstate :]
    step_pre = lax.dot_general(
        dt_proj, dt_low, (((0,), (0,)), ((), ())), preferred_element_type=F32
    )
    step = jax.nn.softplus(step_pre + dt_bias[:, None])
    rates = -jnp.exp(jnp.transpose(a_log))
    old = jnp.where(reset[None, None, :], jnp.zeros((), F32), ssm_state.astype(F32))
    act_wide = activated.astype(F32)
    state = (
        jnp.exp(step[:, None, :] * rates[:, :, None]) * old
        + step[:, None, :] * bmat[None, :, :] * act_wide[:, None, :]
    )
    ssm_new = state.astype(BF16)
    yval = jnp.sum(state * cmat[None, :, :], axis=1) + d_skip[:, None] * act_wide
    gated = (yval * jax.nn.silu(zval.astype(F32))).astype(BF16)

    mixed = lax.dot_general(
        gather_yz(gated).reshape(channels, batch),
        mixer_output,
        (((0,), (0,)), ((), ())),
        preferred_element_type=F32,
    )
    first_out = (
        hidden_in.astype(F32) + scatter_gx(mixed.reshape(gx, batch // gx, width))
    ).astype(BF16)

    first_all = gather_gx(first_out).reshape(batch, width)
    chosen = assign[:, None] == jnp.arange(batch, dtype=jnp.int32)[None, :]
    by_slot = jnp.dot(chosen.astype(BF16), first_all, preferred_element_type=F32)
    squares = jnp.sum(by_slot * by_slot, axis=1)
    gained = (by_slot * norm_gain_b[None, :]).astype(BF16)
    group_count = attention_projection.shape[1]
    group_cols = attention_projection.shape[2]
    flattened = attention_projection.reshape(width, group_count * group_cols)
    slot_count = kv_cache.shape[0]
    entries = jnp.dot(gained, flattened, preferred_element_type=F32)
    extra = jnp.broadcast_to(squares[:, None], (batch, 128))
    entries = jnp.concatenate([entries, extra], axis=1).reshape(yz, slot_count, -1)
    entries = scatter_yz(entries)
    scale = lax.rsqrt(entries[:, -1:] / whole_width + 1e-05)
    newest_entry = (entries[:, :-128] * scale).astype(BF16)
    newest_entry = newest_entry.reshape(slot_count, group_count, group_cols)
    head_dim = kv_cache.shape[3] // 2
    per_group = group_cols // head_dim - 2
    fresh_kv = newest_entry[:, :, per_group * head_dim :]
    query_vector = newest_entry[:, :, : per_group * head_dim].reshape(
        slot_count, group_count, per_group, head_dim
    )
    key_new = newest_entry[:, :, per_group * head_dim : (per_group + 1) * head_dim]
    value_new = newest_entry[:, :, (per_group + 1) * head_dim :]
    keys = kv_cache[..., :head_dim]
    values = kv_cache[..., head_dim:]
    factor = 1.0 / math.sqrt(head_dim)
    scores = (
        jnp.einsum("sghd,stgd->sght", query_vector, keys, preferred_element_type=F32) * factor
    )
    own_score = (
        jnp.einsum("sghd,sgd->sgh", query_vector, key_new, preferred_element_type=F32) * factor
    )
    positions = jnp.arange(kv_cache.shape[1], dtype=jnp.int32)
    valid = (positions[None, :] < lengths[:, None])[:, None, None, :]
    top = jnp.maximum(jnp.max(jnp.where(valid, scores, -1e30), axis=-1), own_score)
    expo = jnp.where(valid, jnp.exp(scores - top[..., None]), 0.0)
    expo_own = jnp.exp(own_score - top)
    total = jnp.sum(expo, axis=-1) + expo_own
    weights = (expo / total[..., None]).astype(BF16)
    weight_own = (expo_own / total).astype(BF16)
    attended = jnp.einsum("sght,stgd->sghd", weights, values, preferred_element_type=F32)
    attended = (
        attended + weight_own.astype(F32)[..., None] * value_new.astype(F32)[:, :, None, :]
    )
    heads = attended.astype(BF16).reshape(slot_count, group_count * per_group * head_dim)
    heads_all = gather_yz(heads).reshape(batch, -1)
    by_request = lax.dot_general(
        chosen.astype(BF16), heads_all, (((0,), (0,)), ((), ())), preferred_element_type=F32
    ).astype(BF16)
    second = jnp.dot(by_request, head_output, preferred_element_type=F32)
    hidden_out = (
        first_out.astype(F32) + scatter_gx(second.reshape(gx, batch // gx, width))
    ).astype(BF16)
    return (hidden_out, ssm_new, conv_new, fresh_kv)


def solution(mesh):
    placed = (
        P(("groups", "gx"), "yz"),
        P("yz"),
        P(None, "gx", "yz"),
        P(None, ("gx", "yz")),
        P(("gx", "yz")),
        P(("gx", "yz"), None, "groups"),
        P(("gx", "yz"), None, "groups"),
        P("groups"),
        P(("gx", "yz"), None),
        P(None, ("gx", "yz")),
        P(("gx", "yz")),
        P(None, ("gx", "yz")),
        P(("gx", "yz")),
        P("gx", "yz"),
        P("yz"),
        P("yz", "gx", None),
        P("gx", "yz"),
        P(("groups", "yz"), None, "gx", None),
        P(("groups", "yz")),
        P("groups"),
    )
    return jax.shard_map(
        on_device,
        mesh=mesh,
        in_specs=placed,
        out_specs=(
            P(("groups", "gx"), "yz"),
            P(("gx", "yz"), None, "groups"),
            P(("gx", "yz"), None, "groups"),
            P(("groups", "yz"), "gx", None),
        ),
        check_vma=False,
    )
```

```python
import math

import jax
import jax.numpy as jnp
from jax import lax
from jax.experimental import pallas as pl
from jax.experimental.pallas import tpu as pltpu
from jax.sharding import PartitionSpec as P

F32 = jnp.float32
BF16 = jnp.bfloat16
MIB = 1 << 20


def swap(value, axis, bits):
    size = lax.axis_size(axis)
    return lax.ppermute(value, axis, [(i, i ^ bits) for i in range(size)])


def swaps_gx(values):
    return [swap(v, "gx", k + 1) for k, v in enumerate(values)]


def swaps_chip(values):
    return [swap(v, "yz", 2 * (k + 1)) for k, v in enumerate(values)]


def gather_yz(value, *staged):
    chips = lax.axis_size("yz") // 2
    got = swaps_chip([value] * (chips - 1))
    *got[1:], staged = lax.optimization_barrier((*got[1:], staged))
    mine = [value] + got
    other = [swap(v, "yz", 1) for v in mine]
    return [v for pair in zip(mine, other) for v in pair], staged


def dot(a, b, dims=((1,), (0,)), **kw):
    return lax.dot_general(a, b, (dims, ((), ())), preferred_element_type=F32, **kw)


def in_hbm(array):
    held = pltpu.with_memory_space_constraint(array, pltpu.HBM)
    return held, pl.BlockSpec(memory_space=pltpu.HBM)


def in_vmem(array):
    held = pltpu.with_memory_space_constraint(array, pltpu.VMEM)
    return held, pl.BlockSpec(memory_space=pltpu.VMEM)


def anywhere(array):
    return array, pl.BlockSpec(memory_space=pl.ANY)


def shape(dims, dtype):
    return pltpu.VMEM(tuple(dims), dtype)


def call(kernel, place, inputs, outs, scratch=(), limit=4, cost=None, name=None):
    pairs = [a if isinstance(a, tuple) else in_vmem(a) for a in inputs]
    return pl.pallas_call(
        kernel,
        grid_spec=pltpu.PrefetchScalarGridSpec(
            num_scalar_prefetch=1,
            grid=(),
            in_specs=[spec for _, spec in pairs],
            out_specs=[pl.BlockSpec(memory_space=pltpu.VMEM)] * len(outs),
            scratch_shapes=list(scratch),
        ),
        out_shape=outs,
        compiler_params=pltpu.CompilerParams(vmem_limit_bytes=limit * MIB),
        cost_estimate=cost and pl.CostEstimate(flops=0, bytes_accessed=cost, transcendentals=0),
        name=name,
    )(place, *[array for array, _ in pairs])


def fetch(pairs, sems):
    copies = [
        pltpu.make_async_copy(source, target, sems.at[k])
        for k, (source, target) in enumerate(pairs)
    ]
    for copy in copies:
        copy.start()
    return copies


def owner_rows(w_ref, half, place_ref, own, target, count):
    return [
        (
            w_ref.at[half, pl.ds(pl.multiple_of(place_ref[k] * own, own), own), :],
            target.at[k],
        )
        for k in range(count)
    ]


def stage_first(place, weights, hidden, gain, own, chips):
    width = weights.shape[2]

    def kernel(place_ref, w_ref, hidden_ref, gain_ref, held, hidden_to, gain_to, sems):
        pairs = owner_rows(w_ref, 0, place_ref, own, held, 2 * chips)
        for copy in fetch(pairs + [(hidden_ref, hidden_to), (gain_ref, gain_to)], sems):
            copy.wait()

    return call(
        kernel,
        place,
        [in_hbm(weights), in_hbm(hidden), in_hbm(gain)],
        [
            shape((2 * chips, own, width), BF16),
            shape(hidden.shape, BF16),
            shape(gain.shape, F32),
        ],
        scratch=[pltpu.SemaphoreType.DMA((2 * chips + 2,))],
        limit=4,
        cost=2 * chips * own * width * 2,
        name="stage_first",
    )


def stage_rows(place, weights, count, earlier, ordered, chips, name):
    rows, width = weights.shape
    block = rows // count

    def kernel(place_ref, w_ref, earlier_ref, held, sems):
        pairs = []
        for k in range(count):
            at = place_ref[2 * chips + 1] ^ k if ordered else k
            pairs.append(
                (w_ref.at[pl.ds(pl.multiple_of(at * block, block), block), :], held.at[k])
            )
        for copy in fetch(pairs, sems):
            copy.wait()

    return call(
        kernel,
        place,
        [in_hbm(weights), anywhere(earlier)],
        [shape((count, block, width), BF16)],
        scratch=[pltpu.SemaphoreType.DMA((count,))],
        limit=4,
        cost=rows * width * 2,
        name=name,
    )[0]


def add_pairs(keep, received, parts, place, name):
    rows = keep.shape[0] // parts
    width = keep.shape[1]

    def kernel(place_ref, keep_ref, received_ref, own_ref, *wire_refs):
        for k in range(parts):
            block = pl.ds(k * rows, rows)
            total = keep_ref[block, :].astype(F32) + received_ref[block, :].astype(F32)
            if k == 0:
                own_ref[...] = total
            else:
                wire_refs[k - 1][...] = total.astype(BF16)

    own, *wires = call(
        kernel,
        place,
        [keep, received],
        [shape((rows, width), F32)] + [shape((rows, width), BF16)] * (parts - 1),
        name=name,
    )
    return own, wires


def add_both(place, part, received, keep, z_received, parts):
    half, batch = part.shape
    own = keep.shape[0] // parts

    def kernel(place_ref, part_ref, received_ref, keep_ref, z_ref, sum_ref, zown_ref, *refs):
        total = part_ref[...] + received_ref[...].astype(F32)
        sum_ref[...] = total
        for k in range(parts):
            block = pl.ds(k * own, own)
            z = keep_ref[block, :].astype(F32) + z_ref[block, :].astype(F32)
            if k == 0:
                zown_ref[...] = z
                continue
            refs[k - 1][:half, :] = total.astype(BF16)
            if k < parts - 1:
                refs[k - 1][half:, :] = z.astype(BF16)
            else:
                refs[k][...] = z.astype(BF16)

    total, zown, *wires = call(
        kernel,
        place,
        [part, received, keep, z_received],
        [shape((half, batch), F32), shape((own, batch), F32)]
        + [shape((half + own, batch), BF16)] * (parts - 2)
        + [shape((half, batch), BF16), shape((own, batch), BF16)],
        name="add_both",
    )
    return total, zown, wires[:-1], wires[-1]


def project_first(place, pieces, gain, weights, batch, chips):
    own, width = weights.shape[1:]
    rows = pieces[0].shape[0]
    count = len(pieces)

    def kernel(place_ref, *refs):
        piece_refs = refs[:count]
        gain_ref, w_ref, out_ref, gained_ref, squares_ref, wide = refs[count:]
        me = place_ref[2 * chips]
        for k in range(count):
            start = pl.multiple_of((me ^ k) * rows, rows)
            wide[pl.ds(start, rows), :] = piece_refs[k][...].astype(F32)
        value = wide[...]
        squares = jnp.sum(value * value, axis=1, keepdims=True)
        squares = jnp.transpose(jnp.broadcast_to(squares, (batch, 128)))[:16, :]
        squares_ref[...] = squares
        gained_ref[...] = jnp.transpose(value * gain_ref[...]).astype(BF16)
        for k in range(chips):
            out_ref[k, :own, :] = dot(w_ref[k], gained_ref[...]).astype(BF16)
            out_ref[k, own:, :] = squares.astype(BF16)

    return call(
        kernel,
        place,
        list(pieces) + [gain, weights],
        [
            shape((chips, own + 16, batch), BF16),
            shape((width, batch), BF16),
            shape((16, batch), F32),
        ],
        scratch=[pltpu.VMEM((batch, width), F32)],
        limit=8,
        name="project_first",
    )


def project_keep(place, weights, gained, squares, chips):
    own = weights.shape[1]
    batch = gained.shape[1]

    def kernel(place_ref, w_ref, gained_ref, squares_ref, out_ref):
        for k in range(chips):
            out_ref[k, :own, :] = dot(w_ref[chips + k], gained_ref[...]).astype(BF16)
            out_ref[k, own:, :] = squares_ref[...].astype(BF16)

    return call(
        kernel,
        place,
        [weights, gained, squares],
        [shape((chips, own + 16, batch), BF16)],
        name="project_keep",
    )[0]


def project_gate(place, weights, gained, conv_rows, x_cols, own, chips, earlier):
    width, batch = gained.shape
    count = 2 * chips

    def kernel(
        place_ref, w_ref, gained_ref, conv_ref, cols_ref, earlier_ref,
        give_ref, keep_ref, conv_to, cols_to, held, sems,
    ):
        pairs = owner_rows(w_ref, 1, place_ref, own, held, count)
        copies = fetch(pairs + [(conv_ref, conv_to), (cols_ref, cols_to)], sems)
        for out_ref, base in ((give_ref, 0), (keep_ref, chips)):
            for k in range(chips):
                copies[base + k].wait()
            for k in range(chips):
                out_ref[k] = dot(held[base + k], gained_ref[...]).astype(BF16)
        copies[count].wait()
        copies[count + 1].wait()

    return call(
        kernel,
        place,
        [in_hbm(weights), gained, in_hbm(conv_rows), in_hbm(x_cols), anywhere(earlier)],
        [shape((chips, own, batch), BF16)] * 2
        + [shape(conv_rows.shape, BF16), shape(x_cols.shape, BF16)],
        scratch=[
            pltpu.VMEM((count, own, width), BF16),
            pltpu.SemaphoreType.DMA((count + 2,)),
        ],
        limit=12,
        cost=count * own * width * 2,
        name="project_gate",
    )


def convolve(place, own_sum, received, conv_state, params, alive, x_cols, own, whole_width):
    taps, _, batch = conv_state.shape
    half = x_cols.shape[0] // 2
    count = len(received)

    def kernel(place_ref, own_ref, *refs):
        got = refs[:count]
        (
            state_ref,
            params_ref,
            alive_ref,
            cols_ref,
            new_ref,
            xa_ref,
            give_ref,
            keep_ref,
            scale_ref,
        ) = refs[count:]
        total = own_ref[...]
        for ref in got:
            total = total + ref[...].astype(F32)
        scale = lax.rsqrt(total[own : own + 8, :] / whole_width + 1e-05)
        scale_ref[...] = scale
        value = (total[:own] * scale[:1]).astype(BF16)
        held = alive_ref[:1, :] > 0
        mixed = params_ref[:, taps : taps + 1] * value.astype(F32)
        for k in range(taps):
            old = jnp.where(held, state_ref[k].astype(F32), 0.0)
            mixed = mixed + params_ref[:, k : k + 1] * old
            if k:
                new_ref[k - 1] = old.astype(BF16)
        new_ref[taps - 1] = value
        mixed = mixed + params_ref[:, taps + 1 : taps + 2]
        active = (mixed / (1.0 + jnp.exp(-mixed))).astype(BF16)
        xa_ref[...] = active
        core = place_ref[place_ref.shape[0] - 1]
        there = pl.multiple_of((1 - core) * half, half)
        here = pl.multiple_of(core * half, half)
        give_ref[...] = dot(cols_ref[pl.ds(there, half), :], active).astype(BF16)
        keep_ref[...] = dot(cols_ref[pl.ds(here, half), :], active)

    return call(
        kernel,
        place,
        [own_sum]
        + list(received)
        + [
            conv_state,
            params,
            alive,
            x_cols,
        ],
        [
            shape(conv_state.shape, BF16),
            shape((own, batch), BF16),
            shape((half, batch), BF16),
            shape((half, batch), F32),
            shape((8, batch), F32),
        ],
        limit=8,
        name="convolve",
    )


def ready_state(place, state, alive, earlier):
    own, nstate, batch = state.shape
    block = 128
    steps, lanes = own // block, batch // 128

    def kernel(place_ref, state_ref, alive_ref, earlier_ref, out_ref, held, wide, sems):
        copies = fetch(
            [(state_ref.at[pl.ds(i * block, block)], held.at[i]) for i in range(steps)], sems
        )
        for i in range(steps):
            copies[i].wait()
            old = held[i].reshape(block * nstate, batch).astype(F32)
            old = jnp.where(alive_ref[:1, :] > 0, old, 0.0)
            for c in range(lanes):
                wide[i % 2, c] = old[:, c * 128 : (c + 1) * 128]
                for n in range(nstate):
                    out_ref[n, i * block : (i + 1) * block, c * 128 : (c + 1) * 128] = wide[
                        i % 2, c, pl.ds(n, block, stride=nstate), :
                    ]

    return call(
        kernel,
        place,
        [in_hbm(state), alive, anywhere(earlier)],
        [shape((nstate, own, batch), F32)],
        scratch=[
            pltpu.VMEM((steps, block, nstate, batch), BF16),
            pltpu.VMEM((2, lanes, block * nstate, 128), F32),
            pltpu.SemaphoreType.DMA((steps,)),
        ],
        limit=16,
        cost=own * nstate * batch * 6,
        name="ready_state",
    )[0]


def scan(place, mine, other, dt_rows, params, state, xa, zown, zgot, scale, taps):
    nstate, own, batch = state.shape
    rank = dt_rows.shape[1]
    half = mine.shape[0]
    block = 128
    steps, lanes = own // block, batch // 128
    count = len(zgot)

    def kernel(place_ref, mine_ref, other_ref, dtw_ref, params_ref, state_ref, *refs):
        xa_ref, zown_ref = refs[:2]
        zrefs = refs[2 : 2 + count]
        scale_ref, new_ref, gated_ref, low, behind, packed, sems = refs[2 + count :]
        core = place_ref[place_ref.shape[0] - 1]
        first = jnp.broadcast_to(core, mine_ref.shape) == 0
        low[:half] = jnp.where(first, mine_ref[...], other_ref[...])
        low[half:] = jnp.where(first, other_ref[...], mine_ref[...])
        copies = []
        for i in range(steps):
            here = slice(i * block, (i + 1) * block)
            pre = dot(dtw_ref[here, :], low[:rank, :]) + params_ref[here, taps + 2 : taps + 3]
            step = jnp.maximum(pre, 0.0) + jnp.log1p(jnp.exp(-jnp.abs(pre)))
            wide = xa_ref[here, :].astype(F32)
            drive = step * wide
            value = params_ref[here, taps + 3 : taps + 4] * wide
            for n in range(nstate):
                rate = params_ref[here, taps + 4 + n : taps + 5 + n]
                bm = low[rank + n : rank + n + 1, :].astype(F32)
                cm = low[rank + nstate + n : rank + nstate + n + 1, :].astype(F32)
                fresh = jnp.exp(-step * rate) * state_ref[n, here, :] + drive * bm
                for c in range(lanes):
                    behind[i % 2, c, pl.ds(n, block, stride=nstate), :] = fresh[
                        :, c * 128 : (c + 1) * 128
                    ]
                value = value + fresh * cm
            for c in range(lanes):
                packed[i, :, :, c * 128 : (c + 1) * 128] = (
                    behind[i % 2, c].reshape(block, nstate, 128).astype(BF16)
                )
            copy = pltpu.make_async_copy(packed.at[i], new_ref.at[pl.ds(i * block, block)], sems.at[i])
            copy.start()
            copies.append(copy)
            ztotal = zown_ref[here, :]
            for ref in zrefs:
                start = ref.shape[0] - own + i * block
                ztotal = ztotal + ref[start : start + block, :].astype(F32)
            gate = (ztotal * scale_ref[:1, :]).astype(BF16).astype(F32)
            value = value * (gate / (1.0 + jnp.exp(-gate)))
            gated_ref[:, here] = jnp.transpose(value).astype(BF16)
        for copy in copies:
            copy.wait()

    pairs = [in_vmem(a) for a in (mine, other, dt_rows, params, state, xa, zown, *zgot, scale)]
    return pl.pallas_call(
        kernel,
        grid_spec=pltpu.PrefetchScalarGridSpec(
            num_scalar_prefetch=1,
            grid=(),
            in_specs=[spec for _, spec in pairs],
            out_specs=[
                pl.BlockSpec(memory_space=pltpu.HBM),
                pl.BlockSpec(memory_space=pltpu.VMEM),
            ],
            scratch_shapes=[
                pltpu.VMEM((2 * half, batch), BF16),
                pltpu.VMEM((2, lanes, block * nstate, 128), F32),
                pltpu.VMEM((steps, block, nstate, batch), BF16),
                pltpu.SemaphoreType.DMA((steps,)),
            ],
        ),
        out_shape=[
            pltpu.HBM((own, nstate, batch), BF16),
            pltpu.VMEM((batch, own), BF16),
        ],
        compiler_params=pltpu.CompilerParams(vmem_limit_bytes=18 * MIB),
        name="scan",
    )(place, *[array for array, _ in pairs])


def mix_out(place, pieces, weights, parts, chips):
    batch, own = pieces[0].shape
    width = weights.shape[2]
    count = len(pieces)
    rows = batch // parts

    def kernel(place_ref, *refs):
        piece_refs = refs[:count]
        w_ref, own_ref = refs[count : count + 2]
        wire_refs = refs[count + 2 : -1]
        total = refs[-1]
        for j in range(count):
            term = dot(piece_refs[j][...], w_ref[j])
            total[...] = term if j == 0 else total[...] + term
        me = place_ref[2 * chips]
        for k in range(parts):
            start = pl.multiple_of((me ^ k) * rows, rows)
            value = total[pl.ds(start, rows), :]
            if k == 0:
                own_ref[...] = value
            else:
                wire_refs[k - 1][...] = value.astype(BF16)

    own_rows, *wires = call(
        kernel,
        place,
        list(pieces) + [weights],
        [shape((rows, width), F32)] + [shape((rows, width), BF16)] * (parts - 1),
        scratch=[pltpu.VMEM((batch, width), F32)],
        limit=8,
        name="mix_out",
    )
    return own_rows, wires


def held_by(assign_ref):
    batch = assign_ref.shape[1]
    requests = lax.broadcasted_iota(jnp.int32, (batch, batch), 0)
    return jnp.where(assign_ref[...] == requests, 1.0, 0.0).astype(BF16)


def query(place, pieces, assign, gain, weights, chips):
    rows, width = pieces[0].shape
    batch = rows * len(pieces)
    count = len(pieces)
    columns = weights.shape[1]
    steps = 5
    block = columns // steps
    half = batch // 2
    slots = half // chips

    def kernel(place_ref, *refs):
        piece_refs = refs[:count]
        assign_ref, gain_ref, w_ref, give_ref, keep_ref, stacked, ordered = refs[count:]
        me = place_ref[2 * chips]
        for k in range(count):
            start = pl.multiple_of((me ^ k) * rows, rows)
            stacked[pl.ds(start, rows), :] = piece_refs[k][...]
        chosen = held_by(assign_ref)
        stacked[...] = dot(chosen, stacked[...], ((0,), (0,))).astype(BF16)
        for k in range(2 * chips):
            start = pl.multiple_of(place_ref[k] * slots, slots)
            ordered[k * slots : (k + 1) * slots, :] = stacked[pl.ds(start, slots), :]
        value = ordered[...].astype(F32)
        squares = jnp.sum(value * value, axis=1, keepdims=True)
        squares = jnp.broadcast_to(squares, (batch, 128)).astype(BF16)
        give_ref[:, columns:] = squares[:half]
        keep_ref[:, columns:] = squares[half:]
        gained = (value * gain_ref[...]).astype(BF16)
        for j in range(steps):
            out = dot(gained, w_ref[:, j * block : (j + 1) * block]).astype(BF16)
            give_ref[:, j * block : (j + 1) * block] = out[:half]
            keep_ref[:, j * block : (j + 1) * block] = out[half:]

    return call(
        kernel,
        place,
        list(pieces) + [assign, gain, weights],
        [shape((half, columns + 128), BF16)] * 2,
        scratch=[pltpu.VMEM((batch, width), BF16)] * 2,
        limit=8,
        name="query",
    )


def head_out(place, pieces, assign, weights, parts, chips):
    slots, depth = pieces[0].shape
    count = len(pieces)
    batch = slots * count
    steps, block, width = weights.shape
    rows = batch // parts

    def kernel(place_ref, *refs):
        piece_refs = refs[:count]
        assign_ref, w_ref, own_ref = refs[count : count + 3]
        wire_refs = refs[count + 3 : -2]
        stacked, total = refs[-2:]
        mine = place_ref[2 * chips + 1]
        for j in range(count):
            start = pl.multiple_of((mine ^ j) * slots, slots)
            stacked[pl.ds(start, slots), :] = piece_refs[j][...]
        chosen = held_by(assign_ref)
        for j in range(steps):
            taken = dot(chosen, stacked[:, j * block : (j + 1) * block]).astype(BF16)
            term = dot(taken, w_ref[j])
            total[...] = term if j == 0 else total[...] + term
        me = place_ref[2 * chips]
        for k in range(parts):
            start = pl.multiple_of((me ^ k) * rows, rows)
            value = total[pl.ds(start, rows), :]
            if k == 0:
                own_ref[...] = value
            else:
                wire_refs[k - 1][...] = value.astype(BF16)

    own_rows, *wires = call(
        kernel,
        place,
        list(pieces) + [assign, weights],
        [shape((rows, width), F32)] + [shape((rows, width), BF16)] * (parts - 1),
        scratch=[pltpu.VMEM((batch, depth), BF16), pltpu.VMEM((batch, width), F32)],
        limit=8,
        name="head_out",
    )
    return own_rows, wires


def total_of(own, received):
    total = own
    for value in received:
        total = total + value.astype(F32)
    return total


def on_device(
    hidden_in,
    norm_gain_a,
    mixer_projection,
    conv_weight,
    conv_bias,
    conv_state,
    ssm_state,
    reset_ids,
    x_proj,
    dt_proj,
    dt_bias,
    a_log,
    d_skip,
    mixer_output,
    norm_gain_b,
    attention_projection,
    head_output,
    kv_cache,
    lengths,
    assign,
):
    batch = assign.shape[0]
    yz, gx = lax.axis_size("yz"), lax.axis_size("gx")
    chips = yz // 2
    me_yz, me_gx = lax.axis_index("yz"), lax.axis_index("gx")
    core = me_yz % 2
    width = hidden_in.shape[1]
    whole_width = width * yz
    own = mixer_projection.shape[1] // yz
    taps = conv_state.shape[1]

    owners = jnp.concatenate(
        [(me_yz ^ 1) ^ (2 * jnp.arange(chips)), me_yz ^ (2 * jnp.arange(chips))]
    ).astype(jnp.int32)
    place = jnp.concatenate([owners, jnp.stack([me_gx, me_yz, core]).astype(jnp.int32)])
    requests = jnp.arange(batch, dtype=jnp.int32)
    x_cols = jnp.transpose(x_proj)
    conv_rows = jnp.transpose(conv_state, (1, 0, 2))
    group_count, group_cols = attention_projection.shape[1:]
    slot_count = kv_cache.shape[0]

    got = swaps_gx([hidden_in] * (gx - 1))
    weights, hidden_here, gain = stage_first(
        place, mixer_projection, hidden_in, norm_gain_a[None, :], own, chips
    )
    got, weights = lax.optimization_barrier((got, weights))
    give, gained, squares = project_first(
        place, [hidden_here] + got, gain, weights, batch, chips
    )
    tall = chips * (own + 16)
    received = swap(give.reshape(tall, batch), "yz", 1)
    keep = project_keep(place, weights, gained, squares, chips)
    xown, wires = add_pairs(keep.reshape(tall, batch), received, chips, place, "add_x")
    xgot = swaps_chip(wires)
    give, keep, conv_rows, x_cols = project_gate(
        place, mixer_projection, gained, conv_rows, x_cols, own, chips, wires[0]
    )
    (conv_weight, a_log, reset_ids, dt_proj), wires = lax.optimization_barrier(
        ((conv_weight, a_log, reset_ids, dt_proj), wires)
    )
    alive = jnp.where(jnp.any(reset_ids[:, None] == requests[None, :], axis=0), 0.0, 1.0)
    alive = jnp.broadcast_to(alive[None, :].astype(F32), (8, batch))
    params = jnp.transpose(
        jnp.concatenate(
            [conv_weight, conv_bias[None], dt_bias[None], d_skip[None], jnp.exp(a_log)], axis=0
        )
    )
    dt_rows = jnp.transpose(dt_proj)
    xgot, give, keep, conv_rows, x_cols, params, alive, dt_rows = lax.optimization_barrier(
        (xgot, give, keep, conv_rows, x_cols, params, alive, dt_rows)
    )
    z_received = swap(give.reshape(chips * own, batch), "yz", 1)
    conv_new, xa, give, part, scale = convolve(
        place, xown, xgot, conv_rows, params, alive, x_cols, own, whole_width
    )
    part, zown, wires, z_last = add_both(
        place, part, swap(give, "yz", 1), keep.reshape(chips * own, batch), z_received, chips
    )
    got = swaps_chip(wires)
    half = part.shape[0]
    part = total_of(part, [g[:half] for g in got])
    z_got = got[:-1] + [swap(z_last, "yz", 2 * (chips - 1))]
    wire = part.astype(BF16)
    got = swaps_gx([wire] * (gx - 1))
    old = ready_state(place, ssm_state, alive, wire)
    got, z_got, old = lax.optimization_barrier((got, z_got, old))
    part = total_of(part, got).astype(BF16)
    ssm_new, gated = scan(
        place, part, swap(part, "yz", 1), dt_rows, params, old, xa, zown, z_got, scale, taps
    )

    gated, attention_projection = lax.optimization_barrier((gated, attention_projection))
    flattened = attention_projection.reshape(width, group_count * group_cols)
    weights = stage_rows(place, mixer_output, yz, gated, True, chips, "stage_mix")
    pieces, (flattened, weights) = gather_yz(gated, flattened, weights)
    own_rows, wires = mix_out(place, pieces, weights, gx, chips)
    first_out = (hidden_in.astype(F32) + total_of(own_rows, swaps_gx(wires))).astype(BF16)

    pieces = [first_out] + swaps_gx([first_out] * (gx - 1))
    give, keep = query(place, pieces, assign[None, :], norm_gain_b[None, :], flattened, chips)
    entries, wires = add_pairs(keep, swap(give, "yz", 1), chips, place, "add_query")
    entries = total_of(entries, swaps_chip(wires))
    scale = lax.rsqrt(entries[:, -1:] / whole_width + 1e-05)
    newest_entry = (entries[:, :-128] * scale).astype(BF16)
    newest_entry = newest_entry.reshape(slot_count, group_count, group_cols)
    head_dim = kv_cache.shape[3] // 2
    per_group = group_cols // head_dim - 2
    fresh_kv = newest_entry[:, :, per_group * head_dim :]
    query_vector = newest_entry[:, :, : per_group * head_dim].reshape(
        slot_count, group_count, per_group, head_dim
    )
    key_new = newest_entry[:, :, per_group * head_dim : (per_group + 1) * head_dim]
    value_new = newest_entry[:, :, (per_group + 1) * head_dim :]
    keys = kv_cache[..., :head_dim]
    values = kv_cache[..., head_dim:]
    factor = 1.0 / math.sqrt(head_dim)
    scores = (
        jnp.einsum("sghd,stgd->sght", query_vector, keys, preferred_element_type=F32) * factor
    )
    own_score = (
        jnp.einsum("sghd,sgd->sgh", query_vector, key_new, preferred_element_type=F32) * factor
    )
    positions = jnp.arange(kv_cache.shape[1], dtype=jnp.int32)
    valid = (positions[None, :] < lengths[:, None])[:, None, None, :]
    top = jnp.maximum(jnp.max(jnp.where(valid, scores, -1e30), axis=-1), own_score)
    expo = jnp.where(valid, jnp.exp(scores - top[..., None]), 0.0)
    expo_own = jnp.exp(own_score - top)
    total = jnp.sum(expo, axis=-1) + expo_own
    weights = (expo / total[..., None]).astype(BF16)
    weight_own = (expo_own / total).astype(BF16)
    attended = jnp.einsum("sght,stgd->sghd", weights, values, preferred_element_type=F32)
    attended = (
        attended + weight_own.astype(F32)[..., None] * value_new.astype(F32)[:, :, None, :]
    )
    heads = attended.astype(BF16).reshape(slot_count, group_count * per_group * head_dim)
    head_weights = stage_rows(place, head_output, 4, heads, False, chips, "stage_head")
    pieces, (head_weights,) = gather_yz(heads, head_weights)
    own_rows, wires = head_out(place, pieces, assign[None, :], head_weights, gx, chips)
    hidden_out = (first_out.astype(F32) + total_of(own_rows, swaps_gx(wires))).astype(BF16)
    return (hidden_out, ssm_new, jnp.transpose(conv_new, (1, 0, 2)), fresh_kv)


def solution(mesh):
    placed = (
        P(("groups", "gx"), "yz"),
        P("yz"),
        P(None, "gx", "yz"),
        P(None, ("gx", "yz")),
        P(("gx", "yz")),
        P(("gx", "yz"), None, "groups"),
        P(("gx", "yz"), None, "groups"),
        P("groups"),
        P(("gx", "yz"), None),
        P(None, ("gx", "yz")),
        P(("gx", "yz")),
        P(None, ("gx", "yz")),
        P(("gx", "yz")),
        P("gx", "yz"),
        P("yz"),
        P("yz", "gx", None),
        P("gx", "yz"),
        P(("groups", "yz"), None, "gx", None),
        P(("groups", "yz")),
        P("groups"),
    )
    return jax.shard_map(
        on_device,
        mesh=mesh,
        in_specs=placed,
        out_specs=(
            P(("groups", "gx"), "yz"),
            P(("gx", "yz"), None, "groups"),
            P(("gx", "yz"), None, "groups"),
            P(("groups", "yz"), "gx", None),
        ),
        check_vma=False,
    )
```

```python
import math

import jax
import jax.numpy as jnp
from jax import lax
from jax.experimental import pallas as pl
from jax.experimental.pallas import tpu as pltpu
from jax.sharding import PartitionSpec as P

F32 = jnp.float32
BF16 = jnp.bfloat16
MIB = 1 << 20


def swap(value, axis, bits):
    size = lax.axis_size(axis)
    return lax.ppermute(value, axis, [(i, i ^ bits) for i in range(size)])


def exchange(values, axis, step, order, depths):
    count = len(values)
    order = [k for k in order if k < count] + [k for k in range(count) if k not in order]
    got = {k: swap(values[k], axis, (k + 1) * step) for k in order}
    for k, depth in enumerate(depths[:count]):
        for _ in range(depth):
            got[k] = lax.optimization_barrier(got[k])
    return [got[k] for k in range(count)]


def swaps_gx(values, order=(2, 0, 1), depths=(1, 0, 2)):
    return exchange(values, "gx", 1, order, depths)


def swaps_chip(values, order=(2, 1, 0), depths=(0, 1, 2)):
    return exchange(values, "yz", 2, order, depths)


def gather_yz(value, got):
    mine = [value] + got
    other = [swap(v, "yz", 1) for v in mine]
    return [v for pair in zip(mine, other) for v in pair]


def dot(a, b, dims=((1,), (0,)), **kw):
    return lax.dot_general(a, b, (dims, ((), ())), preferred_element_type=F32, **kw)


def in_hbm(array):
    held = pltpu.with_memory_space_constraint(array, pltpu.HBM)
    return held, pl.BlockSpec(memory_space=pltpu.HBM)


def in_vmem(array):
    held = pltpu.with_memory_space_constraint(array, pltpu.VMEM)
    return held, pl.BlockSpec(memory_space=pltpu.VMEM)


def anywhere(array):
    return array, pl.BlockSpec(memory_space=pl.ANY)


def shape(dims, dtype):
    return pltpu.VMEM(tuple(dims), dtype)


def call(kernel, place, inputs, outs, scratch=(), limit=4, cost=None, name=None):
    pairs = [a if isinstance(a, tuple) else in_vmem(a) for a in inputs]
    return pl.pallas_call(
        kernel,
        grid_spec=pltpu.PrefetchScalarGridSpec(
            num_scalar_prefetch=1,
            grid=(),
            in_specs=[spec for _, spec in pairs],
            out_specs=[pl.BlockSpec(memory_space=pltpu.VMEM)] * len(outs),
            scratch_shapes=list(scratch),
        ),
        out_shape=outs,
        compiler_params=pltpu.CompilerParams(vmem_limit_bytes=limit * MIB),
        cost_estimate=cost and pl.CostEstimate(flops=0, bytes_accessed=cost, transcendentals=0),
        name=name,
    )(place, *[array for array, _ in pairs])


def fetch(pairs, sems):
    copies = [
        pltpu.make_async_copy(source, target, sems.at[k])
        for k, (source, target) in enumerate(pairs)
    ]
    for copy in copies:
        copy.start()
    return copies


def owner_rows(w_ref, half, place_ref, own, target, count):
    return [
        (
            w_ref.at[half, pl.ds(pl.multiple_of(place_ref[k] * own, own), own), :],
            target.at[k],
        )
        for k in range(count)
    ]


def stage_first(place, weights, hidden, gain, own, chips):
    width = weights.shape[2]

    def kernel(place_ref, w_ref, hidden_ref, gain_ref, held, hidden_to, gain_to, sems):
        pairs = owner_rows(w_ref, 0, place_ref, own, held, 2 * chips)
        for copy in fetch(pairs + [(hidden_ref, hidden_to), (gain_ref, gain_to)], sems):
            copy.wait()

    return call(
        kernel,
        place,
        [in_hbm(weights), in_hbm(hidden), in_hbm(gain)],
        [
            shape((2 * chips, own, width), BF16),
            shape(hidden.shape, BF16),
            shape(gain.shape, F32),
        ],
        scratch=[pltpu.SemaphoreType.DMA((2 * chips + 2,))],
        limit=4,
        cost=2 * chips * own * width * 2,
        name="stage_first",
    )


def stage_rows(place, weights, count, earlier, ordered, chips, name):
    rows, width = weights.shape
    block = rows // count

    def kernel(place_ref, w_ref, earlier_ref, held, sems):
        pairs = []
        for k in range(count):
            at = place_ref[2 * chips + 1] ^ k if ordered else k
            pairs.append(
                (w_ref.at[pl.ds(pl.multiple_of(at * block, block), block), :], held.at[k])
            )
        for copy in fetch(pairs, sems):
            copy.wait()

    return call(
        kernel,
        place,
        [in_hbm(weights), anywhere(earlier)],
        [shape((count, block, width), BF16)],
        scratch=[pltpu.SemaphoreType.DMA((count,))],
        limit=4,
        cost=rows * width * 2,
        name=name,
    )[0]


def add_pairs(keep, received, parts, place, name):
    rows = keep.shape[0] // parts
    width = keep.shape[1]

    def kernel(place_ref, keep_ref, received_ref, own_ref, *wire_refs):
        for k in range(parts):
            block = pl.ds(k * rows, rows)
            total = keep_ref[block, :].astype(F32) + received_ref[block, :].astype(F32)
            if k == 0:
                own_ref[...] = total
            else:
                wire_refs[k - 1][...] = total.astype(BF16)

    own, *wires = call(
        kernel,
        place,
        [keep, received],
        [shape((rows, width), F32)] + [shape((rows, width), BF16)] * (parts - 1),
        name=name,
    )
    return own, wires


def add_both(place, part, received, keep, z_received, parts):
    half, batch = part.shape
    own = keep.shape[0] // parts

    def kernel(place_ref, part_ref, received_ref, keep_ref, z_ref, sum_ref, zown_ref, *refs):
        total = part_ref[...] + received_ref[...].astype(F32)
        sum_ref[...] = total
        for k in range(parts):
            block = pl.ds(k * own, own)
            z = keep_ref[block, :].astype(F32) + z_ref[block, :].astype(F32)
            if k == 0:
                zown_ref[...] = z
                continue
            refs[k - 1][:half, :] = total.astype(BF16)
            if k < parts - 1:
                refs[k - 1][half:, :] = z.astype(BF16)
            else:
                refs[k][...] = z.astype(BF16)

    total, zown, *wires = call(
        kernel,
        place,
        [part, received, keep, z_received],
        [shape((half, batch), F32), shape((own, batch), F32)]
        + [shape((half + own, batch), BF16)] * (parts - 2)
        + [shape((half, batch), BF16), shape((own, batch), BF16)],
        name="add_both",
    )
    return total, zown, wires[:-1], wires[-1]


def project_first(place, pieces, gain, weights, batch, chips):
    own, width = weights.shape[1:]
    rows = pieces[0].shape[0]
    count = len(pieces)

    def kernel(place_ref, *refs):
        piece_refs = refs[:count]
        gain_ref, w_ref, out_ref, gained_ref, squares_ref, wide = refs[count:]
        me = place_ref[2 * chips]
        for k in range(count):
            start = pl.multiple_of((me ^ k) * rows, rows)
            wide[pl.ds(start, rows), :] = piece_refs[k][...].astype(F32)
        value = wide[...]
        squares = jnp.sum(value * value, axis=1, keepdims=True)
        squares = jnp.transpose(jnp.broadcast_to(squares, (batch, 128)))[:16, :]
        squares_ref[...] = squares
        gained_ref[...] = jnp.transpose(value * gain_ref[...]).astype(BF16)
        for k in range(chips):
            out_ref[k, :own, :] = dot(w_ref[k], gained_ref[...]).astype(BF16)
            out_ref[k, own:, :] = squares.astype(BF16)

    return call(
        kernel,
        place,
        list(pieces) + [gain, weights],
        [
            shape((chips, own + 16, batch), BF16),
            shape((width, batch), BF16),
            shape((16, batch), F32),
        ],
        scratch=[pltpu.VMEM((batch, width), F32)],
        limit=8,
        name="project_first",
    )


def project_keep(place, weights, gained, squares, chips):
    own = weights.shape[1]
    batch = gained.shape[1]

    def kernel(place_ref, w_ref, gained_ref, squares_ref, out_ref):
        for k in range(chips):
            out_ref[k, :own, :] = dot(w_ref[chips + k], gained_ref[...]).astype(BF16)
            out_ref[k, own:, :] = squares_ref[...].astype(BF16)

    return call(
        kernel,
        place,
        [weights, gained, squares],
        [shape((chips, own + 16, batch), BF16)],
        name="project_keep",
    )[0]


def project_gate(place, weights, gained, conv_rows, x_cols, own, chips, earlier):
    width, batch = gained.shape
    count = 2 * chips

    def kernel(
        place_ref, w_ref, gained_ref, conv_ref, cols_ref, earlier_ref,
        give_ref, keep_ref, conv_to, cols_to, held, sems,
    ):
        pairs = owner_rows(w_ref, 1, place_ref, own, held, count)
        copies = fetch(pairs + [(conv_ref, conv_to), (cols_ref, cols_to)], sems)
        for out_ref, base in ((give_ref, 0), (keep_ref, chips)):
            for k in range(chips):
                copies[base + k].wait()
            for k in range(chips):
                out_ref[k] = dot(held[base + k], gained_ref[...]).astype(BF16)
        copies[count].wait()
        copies[count + 1].wait()

    return call(
        kernel,
        place,
        [in_hbm(weights), gained, in_hbm(conv_rows), in_hbm(x_cols), anywhere(earlier)],
        [shape((chips, own, batch), BF16)] * 2
        + [shape(conv_rows.shape, BF16), shape(x_cols.shape, BF16)],
        scratch=[
            pltpu.VMEM((count, own, width), BF16),
            pltpu.SemaphoreType.DMA((count + 2,)),
        ],
        limit=12,
        cost=count * own * width * 2,
        name="project_gate",
    )


def convolve(place, own_sum, received, conv_state, params, alive, x_cols, own, whole_width):
    taps, _, batch = conv_state.shape
    half = x_cols.shape[0] // 2
    count = len(received)

    def kernel(place_ref, own_ref, *refs):
        got = refs[:count]
        (
            state_ref,
            params_ref,
            alive_ref,
            cols_ref,
            new_ref,
            xa_ref,
            give_ref,
            keep_ref,
            scale_ref,
        ) = refs[count:]
        total = own_ref[...]
        for ref in got:
            total = total + ref[...].astype(F32)
        scale = lax.rsqrt(total[own : own + 8, :] / whole_width + 1e-05)
        scale_ref[...] = scale
        value = (total[:own] * scale[:1]).astype(BF16)
        held = alive_ref[:1, :] > 0
        mixed = params_ref[:, taps : taps + 1] * value.astype(F32)
        for k in range(taps):
            old = jnp.where(held, state_ref[k].astype(F32), 0.0)
            mixed = mixed + params_ref[:, k : k + 1] * old
            if k:
                new_ref[k - 1] = old.astype(BF16)
        new_ref[taps - 1] = value
        mixed = mixed + params_ref[:, taps + 1 : taps + 2]
        active = (mixed / (1.0 + jnp.exp(-mixed))).astype(BF16)
        xa_ref[...] = active
        core = place_ref[place_ref.shape[0] - 1]
        there = pl.multiple_of((1 - core) * half, half)
        here = pl.multiple_of(core * half, half)
        give_ref[...] = dot(cols_ref[pl.ds(there, half), :], active).astype(BF16)
        keep_ref[...] = dot(cols_ref[pl.ds(here, half), :], active)

    return call(
        kernel,
        place,
        [own_sum]
        + list(received)
        + [
            conv_state,
            params,
            alive,
            x_cols,
        ],
        [
            shape(conv_state.shape, BF16),
            shape((own, batch), BF16),
            shape((half, batch), BF16),
            shape((half, batch), F32),
            shape((8, batch), F32),
        ],
        limit=8,
        name="convolve",
    )


def ready_state(place, state, alive, earlier):
    own, nstate, batch = state.shape
    block = 128
    steps, lanes = own // block, batch // 128

    def kernel(place_ref, state_ref, alive_ref, earlier_ref, out_ref, held, wide, sems):
        copies = fetch(
            [(state_ref.at[pl.ds(i * block, block)], held.at[i]) for i in range(steps)], sems
        )
        for i in range(steps):
            copies[i].wait()
            old = held[i].reshape(block * nstate, batch).astype(F32)
            old = jnp.where(alive_ref[:1, :] > 0, old, 0.0)
            for c in range(lanes):
                wide[i % 2, c] = old[:, c * 128 : (c + 1) * 128]
                for n in range(nstate):
                    out_ref[n, i * block : (i + 1) * block, c * 128 : (c + 1) * 128] = wide[
                        i % 2, c, pl.ds(n, block, stride=nstate), :
                    ]

    return call(
        kernel,
        place,
        [in_hbm(state), alive, anywhere(earlier)],
        [shape((nstate, own, batch), F32)],
        scratch=[
            pltpu.VMEM((steps, block, nstate, batch), BF16),
            pltpu.VMEM((2, lanes, block * nstate, 128), F32),
            pltpu.SemaphoreType.DMA((steps,)),
        ],
        limit=16,
        cost=own * nstate * batch * 6,
        name="ready_state",
    )[0]


def scan(place, mine, other, dt_rows, params, state, xa, zown, zgot, scale, taps):
    nstate, own, batch = state.shape
    rank = dt_rows.shape[1]
    half = mine.shape[0]
    block = 128
    steps, lanes = own // block, batch // 128
    count = len(zgot)

    def kernel(place_ref, mine_ref, other_ref, dtw_ref, params_ref, state_ref, *refs):
        xa_ref, zown_ref = refs[:2]
        zrefs = refs[2 : 2 + count]
        scale_ref, new_ref, gated_ref, low, behind, packed, sems = refs[2 + count :]
        core = place_ref[place_ref.shape[0] - 1]
        first = jnp.broadcast_to(core, mine_ref.shape) == 0
        low[:half] = jnp.where(first, mine_ref[...], other_ref[...])
        low[half:] = jnp.where(first, other_ref[...], mine_ref[...])
        copies = []
        for i in range(steps):
            here = slice(i * block, (i + 1) * block)
            pre = dot(dtw_ref[here, :], low[:rank, :]) + params_ref[here, taps + 2 : taps + 3]
            step = jnp.maximum(pre, 0.0) + jnp.log1p(jnp.exp(-jnp.abs(pre)))
            wide = xa_ref[here, :].astype(F32)
            drive = step * wide
            value = params_ref[here, taps + 3 : taps + 4] * wide
            for n in range(nstate):
                rate = params_ref[here, taps + 4 + n : taps + 5 + n]
                bm = low[rank + n : rank + n + 1, :].astype(F32)
                cm = low[rank + nstate + n : rank + nstate + n + 1, :].astype(F32)
                fresh = jnp.exp(-step * rate) * state_ref[n, here, :] + drive * bm
                for c in range(lanes):
                    behind[i % 2, c, pl.ds(n, block, stride=nstate), :] = fresh[
                        :, c * 128 : (c + 1) * 128
                    ]
                value = value + fresh * cm
            for c in range(lanes):
                packed[i, :, :, c * 128 : (c + 1) * 128] = (
                    behind[i % 2, c].reshape(block, nstate, 128).astype(BF16)
                )
            copy = pltpu.make_async_copy(packed.at[i], new_ref.at[pl.ds(i * block, block)], sems.at[i])
            copy.start()
            copies.append(copy)
            ztotal = zown_ref[here, :]
            for ref in zrefs:
                start = ref.shape[0] - own + i * block
                ztotal = ztotal + ref[start : start + block, :].astype(F32)
            gate = (ztotal * scale_ref[:1, :]).astype(BF16).astype(F32)
            value = value * (gate / (1.0 + jnp.exp(-gate)))
            gated_ref[:, here] = jnp.transpose(value).astype(BF16)
        for copy in copies:
            copy.wait()

    pairs = [in_vmem(a) for a in (mine, other, dt_rows, params, state, xa, zown, *zgot, scale)]
    return pl.pallas_call(
        kernel,
        grid_spec=pltpu.PrefetchScalarGridSpec(
            num_scalar_prefetch=1,
            grid=(),
            in_specs=[spec for _, spec in pairs],
            out_specs=[
                pl.BlockSpec(memory_space=pltpu.HBM),
                pl.BlockSpec(memory_space=pltpu.VMEM),
            ],
            scratch_shapes=[
                pltpu.VMEM((2 * half, batch), BF16),
                pltpu.VMEM((2, lanes, block * nstate, 128), F32),
                pltpu.VMEM((steps, block, nstate, batch), BF16),
                pltpu.SemaphoreType.DMA((steps,)),
            ],
        ),
        out_shape=[
            pltpu.HBM((own, nstate, batch), BF16),
            pltpu.VMEM((batch, own), BF16),
        ],
        compiler_params=pltpu.CompilerParams(vmem_limit_bytes=18 * MIB),
        name="scan",
    )(place, *[array for array, _ in pairs])


def mix_out(place, pieces, weights, parts, chips):
    batch, own = pieces[0].shape
    width = weights.shape[2]
    count = len(pieces)
    rows = batch // parts

    def kernel(place_ref, *refs):
        piece_refs = refs[:count]
        w_ref, own_ref = refs[count : count + 2]
        wire_refs = refs[count + 2 : -1]
        total = refs[-1]
        for j in range(count):
            term = dot(piece_refs[j][...], w_ref[j])
            total[...] = term if j == 0 else total[...] + term
        me = place_ref[2 * chips]
        for k in range(parts):
            start = pl.multiple_of((me ^ k) * rows, rows)
            value = total[pl.ds(start, rows), :]
            if k == 0:
                own_ref[...] = value
            else:
                wire_refs[k - 1][...] = value.astype(BF16)

    own_rows, *wires = call(
        kernel,
        place,
        list(pieces) + [weights],
        [shape((rows, width), F32)] + [shape((rows, width), BF16)] * (parts - 1),
        scratch=[pltpu.VMEM((batch, width), F32)],
        limit=8,
        name="mix_out",
    )
    return own_rows, wires


def held_by(assign_ref):
    batch = assign_ref.shape[1]
    requests = lax.broadcasted_iota(jnp.int32, (batch, batch), 0)
    return jnp.where(assign_ref[...] == requests, 1.0, 0.0).astype(BF16)


def query(place, pieces, assign, gain, weights, chips):
    rows, width = pieces[0].shape
    batch = rows * len(pieces)
    count = len(pieces)
    columns = weights.shape[1]
    steps = 5
    block = columns // steps
    half = batch // 2
    slots = half // chips

    def kernel(place_ref, *refs):
        piece_refs = refs[:count]
        assign_ref, gain_ref, w_ref, give_ref, keep_ref, stacked, ordered = refs[count:]
        me = place_ref[2 * chips]
        for k in range(count):
            start = pl.multiple_of((me ^ k) * rows, rows)
            stacked[pl.ds(start, rows), :] = piece_refs[k][...]
        chosen = held_by(assign_ref)
        stacked[...] = dot(chosen, stacked[...], ((0,), (0,))).astype(BF16)
        for k in range(2 * chips):
            start = pl.multiple_of(place_ref[k] * slots, slots)
            ordered[k * slots : (k + 1) * slots, :] = stacked[pl.ds(start, slots), :]
        value = ordered[...].astype(F32)
        squares = jnp.sum(value * value, axis=1, keepdims=True)
        squares = jnp.broadcast_to(squares, (batch, 128)).astype(BF16)
        give_ref[:, columns:] = squares[:half]
        keep_ref[:, columns:] = squares[half:]
        gained = (value * gain_ref[...]).astype(BF16)
        for j in range(steps):
            out = dot(gained, w_ref[:, j * block : (j + 1) * block]).astype(BF16)
            give_ref[:, j * block : (j + 1) * block] = out[:half]
            keep_ref[:, j * block : (j + 1) * block] = out[half:]

    return call(
        kernel,
        place,
        list(pieces) + [assign, gain, weights],
        [shape((half, columns + 128), BF16)] * 2,
        scratch=[pltpu.VMEM((batch, width), BF16)] * 2,
        limit=8,
        name="query",
    )


def head_out(place, pieces, assign, weights, parts, chips):
    slots, depth = pieces[0].shape
    count = len(pieces)
    batch = slots * count
    steps, block, width = weights.shape
    rows = batch // parts

    def kernel(place_ref, *refs):
        piece_refs = refs[:count]
        assign_ref, w_ref, own_ref = refs[count : count + 3]
        wire_refs = refs[count + 3 : -2]
        stacked, total = refs[-2:]
        mine = place_ref[2 * chips + 1]
        for j in range(count):
            start = pl.multiple_of((mine ^ j) * slots, slots)
            stacked[pl.ds(start, slots), :] = piece_refs[j][...]
        chosen = held_by(assign_ref)
        for j in range(steps):
            taken = dot(chosen, stacked[:, j * block : (j + 1) * block]).astype(BF16)
            term = dot(taken, w_ref[j])
            total[...] = term if j == 0 else total[...] + term
        me = place_ref[2 * chips]
        for k in range(parts):
            start = pl.multiple_of((me ^ k) * rows, rows)
            value = total[pl.ds(start, rows), :]
            if k == 0:
                own_ref[...] = value
            else:
                wire_refs[k - 1][...] = value.astype(BF16)

    own_rows, *wires = call(
        kernel,
        place,
        list(pieces) + [assign, weights],
        [shape((rows, width), F32)] + [shape((rows, width), BF16)] * (parts - 1),
        scratch=[pltpu.VMEM((batch, depth), BF16), pltpu.VMEM((batch, width), F32)],
        limit=8,
        name="head_out",
    )
    return own_rows, wires


def total_of(own, received):
    total = own
    for value in received:
        total = total + value.astype(F32)
    return total


def on_device(
    hidden_in,
    norm_gain_a,
    mixer_projection,
    conv_weight,
    conv_bias,
    conv_state,
    ssm_state,
    reset_ids,
    x_proj,
    dt_proj,
    dt_bias,
    a_log,
    d_skip,
    mixer_output,
    norm_gain_b,
    attention_projection,
    head_output,
    kv_cache,
    lengths,
    assign,
):
    batch = assign.shape[0]
    yz, gx = lax.axis_size("yz"), lax.axis_size("gx")
    chips = yz // 2
    me_yz, me_gx = lax.axis_index("yz"), lax.axis_index("gx")
    core = me_yz % 2
    width = hidden_in.shape[1]
    whole_width = width * yz
    own = mixer_projection.shape[1] // yz
    taps = conv_state.shape[1]

    owners = jnp.concatenate(
        [(me_yz ^ 1) ^ (2 * jnp.arange(chips)), me_yz ^ (2 * jnp.arange(chips))]
    ).astype(jnp.int32)
    place = jnp.concatenate([owners, jnp.stack([me_gx, me_yz, core]).astype(jnp.int32)])
    requests = jnp.arange(batch, dtype=jnp.int32)
    x_cols = jnp.transpose(x_proj)
    conv_rows = jnp.transpose(conv_state, (1, 0, 2))
    group_count, group_cols = attention_projection.shape[1:]
    slot_count = kv_cache.shape[0]

    got = swaps_gx([hidden_in] * (gx - 1), (0, 1, 2), (1, 2, 0))
    weights, hidden_here, gain = stage_first(
        place, mixer_projection, hidden_in, norm_gain_a[None, :], own, chips
    )
    got, weights = lax.optimization_barrier((got, weights))
    give, gained, squares = project_first(
        place, [hidden_here] + got, gain, weights, batch, chips
    )
    tall = chips * (own + 16)
    received = swap(give.reshape(tall, batch), "yz", 1)
    keep = project_keep(place, weights, gained, squares, chips)
    xown, wires = add_pairs(keep.reshape(tall, batch), received, chips, place, "add_x")
    xgot = swaps_chip(wires, (1, 2, 0), (2, 0, 0))
    give, keep, conv_rows, x_cols = project_gate(
        place, mixer_projection, gained, conv_rows, x_cols, own, chips, wires[0]
    )
    (conv_weight, a_log, reset_ids, dt_proj), wires = lax.optimization_barrier(
        ((conv_weight, a_log, reset_ids, dt_proj), wires)
    )
    alive = jnp.where(jnp.any(reset_ids[:, None] == requests[None, :], axis=0), 0.0, 1.0)
    alive = jnp.broadcast_to(alive[None, :].astype(F32), (8, batch))
    params = jnp.transpose(
        jnp.concatenate(
            [conv_weight, conv_bias[None], dt_bias[None], d_skip[None], jnp.exp(a_log)], axis=0
        )
    )
    dt_rows = jnp.transpose(dt_proj)
    xgot, give, keep, conv_rows, x_cols, params, alive, dt_rows = lax.optimization_barrier(
        (xgot, give, keep, conv_rows, x_cols, params, alive, dt_rows)
    )
    z_received = swap(give.reshape(chips * own, batch), "yz", 1)
    conv_new, xa, give, part, scale = convolve(
        place, xown, xgot, conv_rows, params, alive, x_cols, own, whole_width
    )
    part, zown, wires, z_last = add_both(
        place, part, swap(give, "yz", 1), keep.reshape(chips * own, batch), z_received, chips
    )
    got = swaps_chip(wires)
    half = part.shape[0]
    old = ready_state(place, ssm_state, alive, part)
    got, old, z_last = lax.optimization_barrier((got, old, z_last))
    part = total_of(part, [g[:half] for g in got])
    z_got = got[:-1] + [swap(z_last, "yz", 2 * (chips - 1))]
    wire = part.astype(BF16)
    got = swaps_gx([wire] * (gx - 1))
    got, z_got = lax.optimization_barrier((got, z_got))
    part = total_of(part, got).astype(BF16)
    ssm_new, gated = scan(
        place, part, swap(part, "yz", 1), dt_rows, params, old, xa, zown, z_got, scale, taps
    )

    gated, attention_projection = lax.optimization_barrier((gated, attention_projection))
    flattened = attention_projection.reshape(width, group_count * group_cols)
    weights = stage_rows(place, mixer_output, yz, gated, True, chips, "stage_mix")
    got = swaps_chip([gated] * (chips - 1), (0, 1, 2), (0, 0, 0))
    *got[1:], weights, flattened = lax.optimization_barrier((*got[1:], weights, flattened))
    pieces = gather_yz(gated, got)
    own_rows, wires = mix_out(place, pieces, weights, gx, chips)
    first_out = (hidden_in.astype(F32) + total_of(own_rows, swaps_gx(wires))).astype(BF16)

    pieces = [first_out] + swaps_gx([first_out] * (gx - 1))
    give, keep = query(place, pieces, assign[None, :], norm_gain_b[None, :], flattened, chips)
    entries, wires = add_pairs(keep, swap(give, "yz", 1), chips, place, "add_query")
    entries = total_of(entries, swaps_chip(wires, (2, 1, 0), (2, 0, 1)))
    scale = lax.rsqrt(entries[:, -1:] / whole_width + 1e-05)
    newest_entry = (entries[:, :-128] * scale).astype(BF16)
    newest_entry = newest_entry.reshape(slot_count, group_count, group_cols)
    head_dim = kv_cache.shape[3] // 2
    per_group = group_cols // head_dim - 2
    fresh_kv = newest_entry[:, :, per_group * head_dim :]
    query_vector = newest_entry[:, :, : per_group * head_dim].reshape(
        slot_count, group_count, per_group, head_dim
    )
    key_new = newest_entry[:, :, per_group * head_dim : (per_group + 1) * head_dim]
    value_new = newest_entry[:, :, (per_group + 1) * head_dim :]
    keys = kv_cache[..., :head_dim]
    values = kv_cache[..., head_dim:]
    factor = 1.0 / math.sqrt(head_dim)
    scores = (
        jnp.einsum("sghd,stgd->sght", query_vector, keys, preferred_element_type=F32) * factor
    )
    own_score = (
        jnp.einsum("sghd,sgd->sgh", query_vector, key_new, preferred_element_type=F32) * factor
    )
    positions = jnp.arange(kv_cache.shape[1], dtype=jnp.int32)
    valid = (positions[None, :] < lengths[:, None])[:, None, None, :]
    top = jnp.maximum(jnp.max(jnp.where(valid, scores, -1e30), axis=-1), own_score)
    expo = jnp.where(valid, jnp.exp(scores - top[..., None]), 0.0)
    expo_own = jnp.exp(own_score - top)
    total = jnp.sum(expo, axis=-1) + expo_own
    weights = (expo / total[..., None]).astype(BF16)
    weight_own = (expo_own / total).astype(BF16)
    attended = jnp.einsum("sght,stgd->sghd", weights, values, preferred_element_type=F32)
    attended = (
        attended + weight_own.astype(F32)[..., None] * value_new.astype(F32)[:, :, None, :]
    )
    heads = attended.astype(BF16).reshape(slot_count, group_count * per_group * head_dim)
    head_weights = stage_rows(place, head_output, 4, heads, False, chips, "stage_head")
    got = swaps_chip([heads] * (chips - 1), (0, 1, 2), (0, 0, 0))
    got[-1], head_weights = lax.optimization_barrier((got[-1], head_weights))
    pieces = gather_yz(heads, got)
    own_rows, wires = head_out(place, pieces, assign[None, :], head_weights, gx, chips)
    hidden_out = (first_out.astype(F32) + total_of(own_rows, swaps_gx(wires))).astype(BF16)
    return (hidden_out, ssm_new, jnp.transpose(conv_new, (1, 0, 2)), fresh_kv)


def solution(mesh):
    placed = (
        P(("groups", "gx"), "yz"),
        P("yz"),
        P(None, "gx", "yz"),
        P(None, ("gx", "yz")),
        P(("gx", "yz")),
        P(("gx", "yz"), None, "groups"),
        P(("gx", "yz"), None, "groups"),
        P("groups"),
        P(("gx", "yz"), None),
        P(None, ("gx", "yz")),
        P(("gx", "yz")),
        P(None, ("gx", "yz")),
        P(("gx", "yz")),
        P("gx", "yz"),
        P("yz"),
        P("yz", "gx", None),
        P("gx", "yz"),
        P(("groups", "yz"), None, "gx", None),
        P(("groups", "yz")),
        P("groups"),
    )
    return jax.shard_map(
        on_device,
        mesh=mesh,
        in_specs=placed,
        out_specs=(
            P(("groups", "gx"), "yz"),
            P(("gx", "yz"), None, "groups"),
            P(("gx", "yz"), None, "groups"),
            P(("groups", "yz"), "gx", None),
        ),
        check_vma=False,
    )
```

```python
import math

import jax
import jax.numpy as jnp
from jax import lax
from jax.experimental import pallas as pl
from jax.experimental.pallas import tpu as pltpu
from jax.sharding import PartitionSpec as P

F32 = jnp.float32
BF16 = jnp.bfloat16
MIB = 1 << 20


def swap(value, axis, bits):
    size = lax.axis_size(axis)
    return lax.ppermute(value, axis, [(i, i ^ bits) for i in range(size)])


def exchange(values, axis, step, order, depths):
    count = len(values)
    order = [k for k in order if k < count] + [k for k in range(count) if k not in order]
    got = {k: swap(values[k], axis, (k + 1) * step) for k in order}
    for k, depth in enumerate(depths[:count]):
        for _ in range(depth):
            got[k] = lax.optimization_barrier(got[k])
    return [got[k] for k in range(count)]


def swaps_gx(values, order=(2, 0, 1), depths=(1, 0, 2)):
    return exchange(values, "gx", 1, order, depths)


def swaps_chip(values, order=(2, 1, 0), depths=(0, 1, 2)):
    return exchange(values, "yz", 2, order, depths)


def gather_yz(value, got):
    mine = [value] + got
    other = [swap(v, "yz", 1) for v in mine]
    return [v for pair in zip(mine, other) for v in pair]


def dot(a, b, dims=((1,), (0,)), **kw):
    return lax.dot_general(a, b, (dims, ((), ())), preferred_element_type=F32, **kw)


def in_hbm(array):
    held = pltpu.with_memory_space_constraint(array, pltpu.HBM)
    return held, pl.BlockSpec(memory_space=pltpu.HBM)


def in_vmem(array):
    held = pltpu.with_memory_space_constraint(array, pltpu.VMEM)
    return held, pl.BlockSpec(memory_space=pltpu.VMEM)


def anywhere(array):
    return array, pl.BlockSpec(memory_space=pl.ANY)


def shape(dims, dtype):
    return pltpu.VMEM(tuple(dims), dtype)


def call(kernel, place, inputs, outs, scratch=(), limit=4, cost=None, name=None):
    pairs = [a if isinstance(a, tuple) else in_vmem(a) for a in inputs]
    return pl.pallas_call(
        kernel,
        grid_spec=pltpu.PrefetchScalarGridSpec(
            num_scalar_prefetch=1,
            grid=(),
            in_specs=[spec for _, spec in pairs],
            out_specs=[pl.BlockSpec(memory_space=pltpu.VMEM)] * len(outs),
            scratch_shapes=list(scratch),
        ),
        out_shape=outs,
        compiler_params=pltpu.CompilerParams(vmem_limit_bytes=limit * MIB),
        cost_estimate=cost and pl.CostEstimate(flops=0, bytes_accessed=cost, transcendentals=0),
        name=name,
    )(place, *[array for array, _ in pairs])


def fetch(pairs, sems):
    copies = [
        pltpu.make_async_copy(source, target, sems.at[k])
        for k, (source, target) in enumerate(pairs)
    ]
    for copy in copies:
        copy.start()
    return copies


def owner_rows(w_ref, half, place_ref, own, target, count):
    return [
        (
            w_ref.at[half, pl.ds(pl.multiple_of(place_ref[k] * own, own), own), :],
            target.at[k],
        )
        for k in range(count)
    ]


def stage_first(place, weights, hidden, gain, own, chips):
    width = weights.shape[2]

    def kernel(place_ref, w_ref, hidden_ref, gain_ref, held, hidden_to, gain_to, sems):
        pairs = owner_rows(w_ref, 0, place_ref, own, held, 2 * chips)
        for copy in fetch(pairs + [(hidden_ref, hidden_to), (gain_ref, gain_to)], sems):
            copy.wait()

    return call(
        kernel,
        place,
        [in_hbm(weights), in_hbm(hidden), in_hbm(gain)],
        [
            shape((2 * chips, own, width), BF16),
            shape(hidden.shape, BF16),
            shape(gain.shape, F32),
        ],
        scratch=[pltpu.SemaphoreType.DMA((2 * chips + 2,))],
        limit=4,
        cost=2 * chips * own * width * 2,
        name="stage_first",
    )


def stage_rows(place, weights, count, earlier, ordered, chips, name):
    rows, width = weights.shape
    block = rows // count

    def kernel(place_ref, w_ref, earlier_ref, held, sems):
        pairs = []
        for k in range(count):
            at = place_ref[2 * chips + 1] ^ k if ordered else k
            pairs.append(
                (w_ref.at[pl.ds(pl.multiple_of(at * block, block), block), :], held.at[k])
            )
        for copy in fetch(pairs, sems):
            copy.wait()

    return call(
        kernel,
        place,
        [in_hbm(weights), anywhere(earlier)],
        [shape((count, block, width), BF16)],
        scratch=[pltpu.SemaphoreType.DMA((count,))],
        limit=4,
        cost=rows * width * 2,
        name=name,
    )[0]


def add_pairs(keep, received, parts, place, name):
    rows = keep.shape[0] // parts
    width = keep.shape[1]

    def kernel(place_ref, keep_ref, received_ref, own_ref, *wire_refs):
        for k in range(parts):
            block = pl.ds(k * rows, rows)
            total = keep_ref[block, :].astype(F32) + received_ref[block, :].astype(F32)
            if k == 0:
                own_ref[...] = total
            else:
                wire_refs[k - 1][...] = total.astype(BF16)

    own, *wires = call(
        kernel,
        place,
        [keep, received],
        [shape((rows, width), F32)] + [shape((rows, width), BF16)] * (parts - 1),
        name=name,
    )
    return own, wires


def add_both(place, part, received, keep, z_received, parts):
    half, batch = part.shape
    own = keep.shape[0] // parts
    even = parts // 2 * own

    def kernel(place_ref, part_ref, received_ref, keep_ref, z_ref, sum_ref, wire_ref, odd_ref, z_to):
        total = part_ref[...] + received_ref[...].astype(F32)
        sum_ref[...] = total
        wire_ref[...] = total.astype(BF16)
        for k in range(parts):
            block = pl.ds(k * own, own)
            z = keep_ref[block, :].astype(F32) + z_ref[block, :].astype(F32)
            start = k // 2 * own
            if k % 2:
                odd_ref[start : start + own, :] = z.astype(BF16)
            else:
                z_to[start : start + own, :] = z

    return call(
        kernel,
        place,
        [part, received, keep, z_received],
        [
            shape((half, batch), F32),
            shape((half, batch), BF16),
            shape((even, batch), BF16),
            shape((even, batch), F32),
        ],
        name="add_both",
    )


def project_first(place, pieces, gain, weights, batch, chips):
    own, width = weights.shape[1:]
    rows = pieces[0].shape[0]
    count = len(pieces)

    def kernel(place_ref, *refs):
        piece_refs = refs[:count]
        gain_ref, w_ref, out_ref, gained_ref, squares_ref, wide = refs[count:]
        me = place_ref[2 * chips]
        for k in range(count):
            start = pl.multiple_of((me ^ k) * rows, rows)
            wide[pl.ds(start, rows), :] = piece_refs[k][...].astype(F32)
        value = wide[...]
        squares = jnp.sum(value * value, axis=1, keepdims=True)
        squares = jnp.transpose(jnp.broadcast_to(squares, (batch, 128)))[:16, :]
        squares_ref[...] = squares
        gained_ref[...] = jnp.transpose(value * gain_ref[...]).astype(BF16)
        for k in range(chips):
            out_ref[k, :own, :] = dot(w_ref[k], gained_ref[...]).astype(BF16)
            out_ref[k, own:, :] = squares.astype(BF16)

    return call(
        kernel,
        place,
        list(pieces) + [gain, weights],
        [
            shape((chips, own + 16, batch), BF16),
            shape((width, batch), BF16),
            shape((16, batch), F32),
        ],
        scratch=[pltpu.VMEM((batch, width), F32)],
        limit=8,
        name="project_first",
    )


def project_keep(place, weights, gained, squares, chips):
    own = weights.shape[1]
    batch = gained.shape[1]

    def kernel(place_ref, w_ref, gained_ref, squares_ref, out_ref):
        for k in range(chips):
            out_ref[k, :own, :] = dot(w_ref[chips + k], gained_ref[...]).astype(BF16)
            out_ref[k, own:, :] = squares_ref[...].astype(BF16)

    return call(
        kernel,
        place,
        [weights, gained, squares],
        [shape((chips, own + 16, batch), BF16)],
        name="project_keep",
    )[0]


def project_gate(place, weights, gained, conv_rows, x_cols, own, chips, earlier):
    width, batch = gained.shape
    count = 2 * chips

    def kernel(
        place_ref, w_ref, gained_ref, conv_ref, cols_ref, earlier_ref,
        give_ref, keep_ref, conv_to, cols_to, held, sems,
    ):
        pairs = owner_rows(w_ref, 1, place_ref, own, held, count)
        copies = fetch(pairs + [(conv_ref, conv_to), (cols_ref, cols_to)], sems)
        for out_ref, base in ((give_ref, 0), (keep_ref, chips)):
            for k in range(chips):
                copies[base + k].wait()
            for k in range(chips):
                out_ref[k] = dot(held[base + k], gained_ref[...]).astype(BF16)
        copies[count].wait()
        copies[count + 1].wait()

    return call(
        kernel,
        place,
        [in_hbm(weights), gained, in_hbm(conv_rows), in_hbm(x_cols), anywhere(earlier)],
        [shape((chips, own, batch), BF16)] * 2
        + [shape(conv_rows.shape, BF16), shape(x_cols.shape, BF16)],
        scratch=[
            pltpu.VMEM((count, own, width), BF16),
            pltpu.SemaphoreType.DMA((count + 2,)),
        ],
        limit=12,
        cost=count * own * width * 2,
        name="project_gate",
    )


def convolve(place, own_sum, received, conv_state, params, alive, x_cols, own, whole_width):
    taps, _, batch = conv_state.shape
    half = x_cols.shape[0] // 2
    count = len(received)

    def kernel(place_ref, own_ref, *refs):
        got = refs[:count]
        (
            state_ref,
            params_ref,
            alive_ref,
            cols_ref,
            new_ref,
            xa_ref,
            give_ref,
            keep_ref,
            scale_ref,
        ) = refs[count:]
        total = own_ref[...]
        for ref in got:
            total = total + ref[...].astype(F32)
        scale = lax.rsqrt(total[own : own + 8, :] / whole_width + 1e-05)
        scale_ref[...] = scale
        value = (total[:own] * scale[:1]).astype(BF16)
        held = alive_ref[:1, :] > 0
        mixed = params_ref[:, taps : taps + 1] * value.astype(F32)
        for k in range(taps):
            old = jnp.where(held, state_ref[k].astype(F32), 0.0)
            mixed = mixed + params_ref[:, k : k + 1] * old
            if k:
                new_ref[k - 1] = old.astype(BF16)
        new_ref[taps - 1] = value
        mixed = mixed + params_ref[:, taps + 1 : taps + 2]
        active = (mixed / (1.0 + jnp.exp(-mixed))).astype(BF16)
        xa_ref[...] = active
        core = place_ref[place_ref.shape[0] - 1]
        there = pl.multiple_of((1 - core) * half, half)
        here = pl.multiple_of(core * half, half)
        give_ref[...] = dot(cols_ref[pl.ds(there, half), :], active).astype(BF16)
        keep_ref[...] = dot(cols_ref[pl.ds(here, half), :], active)

    return call(
        kernel,
        place,
        [own_sum]
        + list(received)
        + [
            conv_state,
            params,
            alive,
            x_cols,
        ],
        [
            shape(conv_state.shape, BF16),
            shape((own, batch), BF16),
            shape((half, batch), BF16),
            shape((half, batch), F32),
            shape((8, batch), F32),
        ],
        limit=8,
        name="convolve",
    )


def ready_state(place, state, alive, earlier):
    own, nstate, batch = state.shape
    block = 128
    steps, lanes = own // block, batch // 128

    def kernel(place_ref, state_ref, alive_ref, earlier_ref, out_ref, held, wide, sems):
        copies = fetch(
            [(state_ref.at[pl.ds(i * block, block)], held.at[i]) for i in range(steps)], sems
        )
        for i in range(steps):
            copies[i].wait()
            old = held[i].reshape(block * nstate, batch).astype(F32)
            old = jnp.where(alive_ref[:1, :] > 0, old, 0.0)
            for c in range(lanes):
                wide[i % 2, c] = old[:, c * 128 : (c + 1) * 128]
                for n in range(nstate):
                    out_ref[n, i * block : (i + 1) * block, c * 128 : (c + 1) * 128] = wide[
                        i % 2, c, pl.ds(n, block, stride=nstate), :
                    ]

    return call(
        kernel,
        place,
        [in_hbm(state), alive, anywhere(earlier)],
        [shape((nstate, own, batch), F32)],
        scratch=[
            pltpu.VMEM((steps, block, nstate, batch), BF16),
            pltpu.VMEM((2, lanes, block * nstate, 128), F32),
            pltpu.SemaphoreType.DMA((steps,)),
        ],
        limit=16,
        cost=own * nstate * batch * 6,
        name="ready_state",
    )[0]


def scan(place, mine, other, dt_rows, params, state, xa, taps):
    nstate, own, batch = state.shape
    rank = dt_rows.shape[1]
    half = mine.shape[0]
    block = 128
    steps, lanes = own // block, batch // 128

    def kernel(place_ref, mine_ref, other_ref, dtw_ref, params_ref, state_ref, *refs):
        xa_ref, new_ref, value_ref, low, behind, packed, sems = refs
        core = place_ref[place_ref.shape[0] - 1]
        first = jnp.broadcast_to(core, mine_ref.shape) == 0
        low[:half] = jnp.where(first, mine_ref[...], other_ref[...])
        low[half:] = jnp.where(first, other_ref[...], mine_ref[...])
        copies = []
        for i in range(steps):
            here = slice(i * block, (i + 1) * block)
            pre = dot(dtw_ref[here, :], low[:rank, :]) + params_ref[here, taps + 2 : taps + 3]
            step = jnp.maximum(pre, 0.0) + jnp.log1p(jnp.exp(-jnp.abs(pre)))
            wide = xa_ref[here, :].astype(F32)
            drive = step * wide
            value = params_ref[here, taps + 3 : taps + 4] * wide
            for n in range(nstate):
                rate = params_ref[here, taps + 4 + n : taps + 5 + n]
                bm = low[rank + n : rank + n + 1, :].astype(F32)
                cm = low[rank + nstate + n : rank + nstate + n + 1, :].astype(F32)
                fresh = jnp.exp(-step * rate) * state_ref[n, here, :] + drive * bm
                for c in range(lanes):
                    behind[i % 2, c, pl.ds(n, block, stride=nstate), :] = fresh[
                        :, c * 128 : (c + 1) * 128
                    ]
                value = value + fresh * cm
            for c in range(lanes):
                packed[i, :, :, c * 128 : (c + 1) * 128] = (
                    behind[i % 2, c].reshape(block, nstate, 128).astype(BF16)
                )
            copy = pltpu.make_async_copy(packed.at[i], new_ref.at[pl.ds(i * block, block)], sems.at[i])
            copy.start()
            copies.append(copy)
            value_ref[here, :] = value
        for copy in copies:
            copy.wait()

    pairs = [in_vmem(a) for a in (mine, other, dt_rows, params, state, xa)]
    return pl.pallas_call(
        kernel,
        grid_spec=pltpu.PrefetchScalarGridSpec(
            num_scalar_prefetch=1,
            grid=(),
            in_specs=[spec for _, spec in pairs],
            out_specs=[
                pl.BlockSpec(memory_space=pltpu.HBM),
                pl.BlockSpec(memory_space=pltpu.VMEM),
            ],
            scratch_shapes=[
                pltpu.VMEM((2 * half, batch), BF16),
                pltpu.VMEM((2, lanes, block * nstate, 128), F32),
                pltpu.VMEM((steps, block, nstate, batch), BF16),
                pltpu.SemaphoreType.DMA((steps,)),
            ],
        ),
        out_shape=[
            pltpu.HBM((own, nstate, batch), BF16),
            pltpu.VMEM((own, batch), F32),
        ],
        compiler_params=pltpu.CompilerParams(vmem_limit_bytes=18 * MIB),
        cost_estimate=pl.CostEstimate(flops=0, bytes_accessed=1, transcendentals=0),
        name="scan",
    )(place, *[array for array, _ in pairs])


def gate_rows(place, value, zown, zgot, scale):
    own, batch = value.shape
    count = len(zgot)

    def kernel(place_ref, value_ref, zown_ref, *refs):
        scale_ref, gated_ref = refs[count:]
        total = zown_ref[...]
        for ref in refs[:count]:
            total = total + ref[...].astype(F32)
        gate = (total * scale_ref[:1, :]).astype(BF16).astype(F32)
        value = value_ref[...] * (gate / (1.0 + jnp.exp(-gate)))
        gated_ref[...] = jnp.transpose(value).astype(BF16)

    return call(
        kernel,
        place,
        [value, zown, *zgot, scale],
        [shape((batch, own), BF16)],
        name="gate_rows",
    )[0]


def mix_out(place, pieces, weights, parts, chips):
    batch, own = pieces[0].shape
    width = weights.shape[2]
    count = len(pieces)
    rows = batch // parts

    def kernel(place_ref, *refs):
        piece_refs = refs[:count]
        w_ref, own_ref = refs[count : count + 2]
        wire_refs = refs[count + 2 : -1]
        total = refs[-1]
        for j in range(count):
            term = dot(piece_refs[j][...], w_ref[j])
            total[...] = term if j == 0 else total[...] + term
        me = place_ref[2 * chips]
        for k in range(parts):
            start = pl.multiple_of((me ^ k) * rows, rows)
            value = total[pl.ds(start, rows), :]
            if k == 0:
                own_ref[...] = value
            else:
                wire_refs[k - 1][...] = value.astype(BF16)

    own_rows, *wires = call(
        kernel,
        place,
        list(pieces) + [weights],
        [shape((rows, width), F32)] + [shape((rows, width), BF16)] * (parts - 1),
        scratch=[pltpu.VMEM((batch, width), F32)],
        limit=8,
        name="mix_out",
    )
    return own_rows, wires


def held_by(assign_ref):
    batch = assign_ref.shape[1]
    requests = lax.broadcasted_iota(jnp.int32, (batch, batch), 0)
    return jnp.where(assign_ref[...] == requests, 1.0, 0.0).astype(BF16)


def query(place, pieces, assign, gain, weights, chips):
    rows, width = pieces[0].shape
    batch = rows * len(pieces)
    count = len(pieces)
    columns = weights.shape[1]
    steps = 5
    block = columns // steps
    half = batch // 2
    slots = half // chips

    def kernel(place_ref, *refs):
        piece_refs = refs[:count]
        assign_ref, gain_ref, w_ref, give_ref, keep_ref, stacked, ordered = refs[count:]
        me = place_ref[2 * chips]
        for k in range(count):
            start = pl.multiple_of((me ^ k) * rows, rows)
            stacked[pl.ds(start, rows), :] = piece_refs[k][...]
        chosen = held_by(assign_ref)
        stacked[...] = dot(chosen, stacked[...], ((0,), (0,))).astype(BF16)
        for k in range(2 * chips):
            start = pl.multiple_of(place_ref[k] * slots, slots)
            ordered[k * slots : (k + 1) * slots, :] = stacked[pl.ds(start, slots), :]
        value = ordered[...].astype(F32)
        squares = jnp.sum(value * value, axis=1, keepdims=True)
        squares = jnp.broadcast_to(squares, (batch, 128)).astype(BF16)
        give_ref[:, columns:] = squares[:half]
        keep_ref[:, columns:] = squares[half:]
        gained = (value * gain_ref[...]).astype(BF16)
        for j in range(steps):
            out = dot(gained, w_ref[:, j * block : (j + 1) * block]).astype(BF16)
            give_ref[:, j * block : (j + 1) * block] = out[:half]
            keep_ref[:, j * block : (j + 1) * block] = out[half:]

    return call(
        kernel,
        place,
        list(pieces) + [assign, gain, weights],
        [shape((half, columns + 128), BF16)] * 2,
        scratch=[pltpu.VMEM((batch, width), BF16)] * 2,
        limit=8,
        name="query",
    )


def head_out(place, pieces, assign, weights, parts, chips):
    slots, depth = pieces[0].shape
    count = len(pieces)
    batch = slots * count
    steps, block, width = weights.shape
    rows = batch // parts

    def kernel(place_ref, *refs):
        piece_refs = refs[:count]
        assign_ref, w_ref, own_ref = refs[count : count + 3]
        wire_refs = refs[count + 3 : -2]
        stacked, total = refs[-2:]
        mine = place_ref[2 * chips + 1]
        for j in range(count):
            start = pl.multiple_of((mine ^ j) * slots, slots)
            stacked[pl.ds(start, slots), :] = piece_refs[j][...]
        chosen = held_by(assign_ref)
        for j in range(steps):
            taken = dot(chosen, stacked[:, j * block : (j + 1) * block]).astype(BF16)
            term = dot(taken, w_ref[j])
            total[...] = term if j == 0 else total[...] + term
        me = place_ref[2 * chips]
        for k in range(parts):
            start = pl.multiple_of((me ^ k) * rows, rows)
            value = total[pl.ds(start, rows), :]
            if k == 0:
                own_ref[...] = value
            else:
                wire_refs[k - 1][...] = value.astype(BF16)

    own_rows, *wires = call(
        kernel,
        place,
        list(pieces) + [assign, weights],
        [shape((rows, width), F32)] + [shape((rows, width), BF16)] * (parts - 1),
        scratch=[pltpu.VMEM((batch, depth), BF16), pltpu.VMEM((batch, width), F32)],
        limit=8,
        name="head_out",
    )
    return own_rows, wires


def total_of(own, received):
    total = own
    for value in received:
        total = total + value.astype(F32)
    return total


def on_device(
    hidden_in,
    norm_gain_a,
    mixer_projection,
    conv_weight,
    conv_bias,
    conv_state,
    ssm_state,
    reset_ids,
    x_proj,
    dt_proj,
    dt_bias,
    a_log,
    d_skip,
    mixer_output,
    norm_gain_b,
    attention_projection,
    head_output,
    kv_cache,
    lengths,
    assign,
):
    batch = assign.shape[0]
    yz, gx = lax.axis_size("yz"), lax.axis_size("gx")
    chips = yz // 2
    me_yz, me_gx = lax.axis_index("yz"), lax.axis_index("gx")
    core = me_yz % 2
    width = hidden_in.shape[1]
    whole_width = width * yz
    own = mixer_projection.shape[1] // yz
    taps = conv_state.shape[1]

    owners = jnp.concatenate(
        [(me_yz ^ 1) ^ (2 * jnp.arange(chips)), me_yz ^ (2 * jnp.arange(chips))]
    ).astype(jnp.int32)
    place = jnp.concatenate([owners, jnp.stack([me_gx, me_yz, core]).astype(jnp.int32)])
    requests = jnp.arange(batch, dtype=jnp.int32)
    x_cols = jnp.transpose(x_proj)
    conv_rows = jnp.transpose(conv_state, (1, 0, 2))
    group_count, group_cols = attention_projection.shape[1:]
    slot_count = kv_cache.shape[0]

    got = swaps_gx([hidden_in] * (gx - 1), (0, 1, 2), (1, 2, 0))
    weights, hidden_here, gain = stage_first(
        place, mixer_projection, hidden_in, norm_gain_a[None, :], own, chips
    )
    got, weights = lax.optimization_barrier((got, weights))
    give, gained, squares = project_first(
        place, [hidden_here] + got, gain, weights, batch, chips
    )
    tall = chips * (own + 16)
    received = swap(give.reshape(tall, batch), "yz", 1)
    keep = project_keep(place, weights, gained, squares, chips)
    xown, wires = add_pairs(keep.reshape(tall, batch), received, chips, place, "add_x")
    xgot = swaps_chip(wires, (1, 2, 0), (2, 0, 0))
    give, keep, conv_rows, x_cols = project_gate(
        place, mixer_projection, gained, conv_rows, x_cols, own, chips, wires[0]
    )
    (conv_weight, a_log, reset_ids, dt_proj), wires = lax.optimization_barrier(
        ((conv_weight, a_log, reset_ids, dt_proj), wires)
    )
    alive = jnp.where(jnp.any(reset_ids[:, None] == requests[None, :], axis=0), 0.0, 1.0)
    alive = jnp.broadcast_to(alive[None, :].astype(F32), (8, batch))
    params = jnp.transpose(
        jnp.concatenate(
            [conv_weight, conv_bias[None], dt_bias[None], d_skip[None], jnp.exp(a_log)], axis=0
        )
    )
    dt_rows = jnp.transpose(dt_proj)
    xgot, give, keep, conv_rows, x_cols, params, alive, dt_rows = lax.optimization_barrier(
        (xgot, give, keep, conv_rows, x_cols, params, alive, dt_rows)
    )
    z_received = swap(give.reshape(chips * own, batch), "yz", 1)
    conv_new, xa, give, part, scale = convolve(
        place, xown, xgot, conv_rows, params, alive, x_cols, own, whole_width
    )
    part, wire, z_odd, z_even = add_both(
        place, part, swap(give, "yz", 1), keep.reshape(chips * own, batch), z_received, chips
    )
    got = swaps_chip([wire] * (chips - 1), (2, 1, 0), (2, 1, 0))
    z_near = swap(z_odd, "yz", 2)
    old = ready_state(place, ssm_state, alive, part)
    got, old = lax.optimization_barrier((got, old))
    part = total_of(part, got)
    wire = part.astype(BF16)
    got = swaps_gx([wire] * (gx - 1), (0, 1, 2), (0, 0, 0))
    z_even = z_even + z_near.astype(F32)
    z_wires = [z_even[k * own : (k + 1) * own].astype(BF16) for k in range(1, chips // 2)]
    z_got = [swap(w, "yz", 4 * (k + 1)) for k, w in enumerate(z_wires)]
    part = total_of(part, got).astype(BF16)
    ssm_new, value = scan(
        place, part, swap(part, "yz", 1), dt_rows, params, old, xa, taps
    )
    gated = gate_rows(place, value, z_even[:own], z_got, scale)

    gated, attention_projection = lax.optimization_barrier((gated, attention_projection))
    flattened = attention_projection.reshape(width, group_count * group_cols)
    weights = stage_rows(place, mixer_output, yz, gated, True, chips, "stage_mix")
    got = swaps_chip([gated] * (chips - 1), (0, 1, 2), (0, 0, 0))
    *got[1:], weights, flattened = lax.optimization_barrier((*got[1:], weights, flattened))
    pieces = gather_yz(gated, got)
    own_rows, wires = mix_out(place, pieces, weights, gx, chips)
    first_out = (hidden_in.astype(F32) + total_of(own_rows, swaps_gx(wires))).astype(BF16)

    pieces = [first_out] + swaps_gx([first_out] * (gx - 1))
    give, keep = query(place, pieces, assign[None, :], norm_gain_b[None, :], flattened, chips)
    entries, wires = add_pairs(keep, swap(give, "yz", 1), chips, place, "add_query")
    entries = total_of(entries, swaps_chip(wires, (2, 1, 0), (2, 0, 1)))
    scale = lax.rsqrt(entries[:, -1:] / whole_width + 1e-05)
    newest_entry = (entries[:, :-128] * scale).astype(BF16)
    newest_entry = newest_entry.reshape(slot_count, group_count, group_cols)
    head_dim = kv_cache.shape[3] // 2
    per_group = group_cols // head_dim - 2
    fresh_kv = newest_entry[:, :, per_group * head_dim :]
    query_vector = newest_entry[:, :, : per_group * head_dim].reshape(
        slot_count, group_count, per_group, head_dim
    )
    key_new = newest_entry[:, :, per_group * head_dim : (per_group + 1) * head_dim]
    value_new = newest_entry[:, :, (per_group + 1) * head_dim :]
    keys = kv_cache[..., :head_dim]
    values = kv_cache[..., head_dim:]
    factor = 1.0 / math.sqrt(head_dim)
    scores = (
        jnp.einsum("sghd,stgd->sght", query_vector, keys, preferred_element_type=F32) * factor
    )
    own_score = (
        jnp.einsum("sghd,sgd->sgh", query_vector, key_new, preferred_element_type=F32) * factor
    )
    positions = jnp.arange(kv_cache.shape[1], dtype=jnp.int32)
    valid = (positions[None, :] < lengths[:, None])[:, None, None, :]
    top = jnp.maximum(jnp.max(jnp.where(valid, scores, -1e30), axis=-1), own_score)
    expo = jnp.where(valid, jnp.exp(scores - top[..., None]), 0.0)
    expo_own = jnp.exp(own_score - top)
    total = jnp.sum(expo, axis=-1) + expo_own
    weights = (expo / total[..., None]).astype(BF16)
    weight_own = (expo_own / total).astype(BF16)
    attended = jnp.einsum("sght,stgd->sghd", weights, values, preferred_element_type=F32)
    attended = (
        attended + weight_own.astype(F32)[..., None] * value_new.astype(F32)[:, :, None, :]
    )
    heads = attended.astype(BF16).reshape(slot_count, group_count * per_group * head_dim)
    head_weights = stage_rows(place, head_output, 4, heads, False, chips, "stage_head")
    got = swaps_chip([heads] * (chips - 1), (0, 1, 2), (0, 0, 0))
    got[-1], head_weights = lax.optimization_barrier((got[-1], head_weights))
    pieces = gather_yz(heads, got)
    own_rows, wires = head_out(place, pieces, assign[None, :], head_weights, gx, chips)
    hidden_out = (first_out.astype(F32) + total_of(own_rows, swaps_gx(wires))).astype(BF16)
    return (hidden_out, ssm_new, jnp.transpose(conv_new, (1, 0, 2)), fresh_kv)


def solution(mesh):
    placed = (
        P(("groups", "gx"), "yz"),
        P("yz"),
        P(None, "gx", "yz"),
        P(None, ("gx", "yz")),
        P(("gx", "yz")),
        P(("gx", "yz"), None, "groups"),
        P(("gx", "yz"), None, "groups"),
        P("groups"),
        P(("gx", "yz"), None),
        P(None, ("gx", "yz")),
        P(("gx", "yz")),
        P(None, ("gx", "yz")),
        P(("gx", "yz")),
        P("gx", "yz"),
        P("yz"),
        P("yz", "gx", None),
        P("gx", "yz"),
        P(("groups", "yz"), None, "gx", None),
        P(("groups", "yz")),
        P("groups"),
    )
    return jax.shard_map(
        on_device,
        mesh=mesh,
        in_specs=placed,
        out_specs=(
            P(("groups", "gx"), "yz"),
            P(("gx", "yz"), None, "groups"),
            P(("gx", "yz"), None, "groups"),
            P(("groups", "yz"), "gx", None),
        ),
        check_vma=False,
    )
```

```python
import math

import jax
import jax.numpy as jnp
from jax import lax
from jax.experimental import pallas as pl
from jax.experimental.pallas import tpu as pltpu
from jax.sharding import PartitionSpec as P

F32 = jnp.float32
BF16 = jnp.bfloat16
MIB = 1 << 20


def swap(value, axis, bits):
    size = lax.axis_size(axis)
    return lax.ppermute(value, axis, [(i, i ^ bits) for i in range(size)])


def exchange(values, axis, step, order, depths):
    count = len(values)
    order = [k for k in order if k < count] + [k for k in range(count) if k not in order]
    got = {k: swap(values[k], axis, (k + 1) * step) for k in order}
    for k, depth in enumerate(depths[:count]):
        for _ in range(depth):
            got[k] = lax.optimization_barrier(got[k])
    return [got[k] for k in range(count)]


def swaps_gx(values, order=(2, 0, 1), depths=(1, 0, 2)):
    return exchange(values, "gx", 1, order, depths)


def swaps_chip(values, order=(2, 1, 0), depths=(0, 1, 2)):
    return exchange(values, "yz", 2, order, depths)


def gather_yz(value, got):
    mine = [value] + got
    other = [swap(v, "yz", 1) for v in mine]
    return [v for pair in zip(mine, other) for v in pair]


def dot(a, b, dims=((1,), (0,)), **kw):
    return lax.dot_general(a, b, (dims, ((), ())), preferred_element_type=F32, **kw)


def in_hbm(array):
    held = pltpu.with_memory_space_constraint(array, pltpu.HBM)
    return held, pl.BlockSpec(memory_space=pltpu.HBM)


def in_vmem(array):
    held = pltpu.with_memory_space_constraint(array, pltpu.VMEM)
    return held, pl.BlockSpec(memory_space=pltpu.VMEM)


def anywhere(array):
    return array, pl.BlockSpec(memory_space=pl.ANY)


def shape(dims, dtype):
    return pltpu.VMEM(tuple(dims), dtype)


def call(kernel, place, inputs, outs, scratch=(), limit=4, cost=None, name=None):
    pairs = [a if isinstance(a, tuple) else in_vmem(a) for a in inputs]
    return pl.pallas_call(
        kernel,
        grid_spec=pltpu.PrefetchScalarGridSpec(
            num_scalar_prefetch=1,
            grid=(),
            in_specs=[spec for _, spec in pairs],
            out_specs=[pl.BlockSpec(memory_space=pltpu.VMEM)] * len(outs),
            scratch_shapes=list(scratch),
        ),
        out_shape=outs,
        compiler_params=pltpu.CompilerParams(vmem_limit_bytes=limit * MIB),
        cost_estimate=cost and pl.CostEstimate(flops=0, bytes_accessed=cost, transcendentals=0),
        name=name,
    )(place, *[array for array, _ in pairs])


def fetch(pairs, sems):
    copies = [
        pltpu.make_async_copy(source, target, sems.at[k])
        for k, (source, target) in enumerate(pairs)
    ]
    for copy in copies:
        copy.start()
    return copies


def owner_rows(w_ref, half, place_ref, own, target, count):
    return [
        (
            w_ref.at[half, pl.ds(pl.multiple_of(place_ref[k] * own, own), own), :],
            target.at[k],
        )
        for k in range(count)
    ]


def stage_first(place, weights, hidden, gain, own, chips):
    width = weights.shape[2]

    def kernel(place_ref, w_ref, hidden_ref, gain_ref, held, hidden_to, gain_to, sems):
        pairs = owner_rows(w_ref, 0, place_ref, own, held, 2 * chips)
        for copy in fetch(pairs + [(hidden_ref, hidden_to), (gain_ref, gain_to)], sems):
            copy.wait()

    return call(
        kernel,
        place,
        [in_hbm(weights), in_hbm(hidden), in_hbm(gain)],
        [
            shape((2 * chips, own, width), BF16),
            shape(hidden.shape, BF16),
            shape(gain.shape, F32),
        ],
        scratch=[pltpu.SemaphoreType.DMA((2 * chips + 2,))],
        limit=4,
        cost=2 * chips * own * width * 2,
        name="stage_first",
    )


def stage_rows(place, weights, count, earlier, ordered, chips, name):
    rows, width = weights.shape
    block = rows // count

    def kernel(place_ref, w_ref, earlier_ref, held, sems):
        pairs = []
        for k in range(count):
            at = place_ref[2 * chips + 1] ^ k if ordered else k
            pairs.append(
                (w_ref.at[pl.ds(pl.multiple_of(at * block, block), block), :], held.at[k])
            )
        for copy in fetch(pairs, sems):
            copy.wait()

    return call(
        kernel,
        place,
        [in_hbm(weights), anywhere(earlier)],
        [shape((count, block, width), BF16)],
        scratch=[pltpu.SemaphoreType.DMA((count,))],
        limit=4,
        cost=rows * width * 2,
        name=name,
    )[0]


def add_pairs(keep, received, parts, place, name):
    rows = keep.shape[0] // parts
    width = keep.shape[1]

    def kernel(place_ref, keep_ref, received_ref, own_ref, *wire_refs):
        for k in range(parts):
            block = pl.ds(k * rows, rows)
            total = keep_ref[block, :].astype(F32) + received_ref[block, :].astype(F32)
            if k == 0:
                own_ref[...] = total
            else:
                wire_refs[k - 1][...] = total.astype(BF16)

    own, *wires = call(
        kernel,
        place,
        [keep, received],
        [shape((rows, width), F32)] + [shape((rows, width), BF16)] * (parts - 1),
        name=name,
    )
    return own, wires


def add_both(place, part, received, keep, z_received, parts):
    half, batch = part.shape
    own = keep.shape[0] // parts
    even = parts // 2 * own

    def kernel(place_ref, part_ref, received_ref, keep_ref, z_ref, sum_ref, wire_ref, odd_ref, z_to):
        total = part_ref[...] + received_ref[...].astype(F32)
        sum_ref[...] = total
        wire_ref[...] = total.astype(BF16)
        for k in range(parts):
            block = pl.ds(k * own, own)
            z = keep_ref[block, :].astype(F32) + z_ref[block, :].astype(F32)
            start = k // 2 * own
            if k % 2:
                odd_ref[start : start + own, :] = z.astype(BF16)
            else:
                z_to[start : start + own, :] = z

    return call(
        kernel,
        place,
        [part, received, keep, z_received],
        [
            shape((half, batch), F32),
            shape((half, batch), BF16),
            shape((even, batch), BF16),
            shape((even, batch), F32),
        ],
        name="add_both",
    )


def project_first(place, pieces, gain, weights, batch, chips):
    own, width = weights.shape[1:]
    rows = pieces[0].shape[0]
    count = len(pieces)

    def kernel(place_ref, *refs):
        piece_refs = refs[:count]
        gain_ref, w_ref, out_ref, gained_ref, squares_ref, wide = refs[count:]
        me = place_ref[2 * chips]
        for k in range(count):
            start = pl.multiple_of((me ^ k) * rows, rows)
            wide[pl.ds(start, rows), :] = piece_refs[k][...].astype(F32)
        value = wide[...]
        squares = jnp.sum(value * value, axis=1, keepdims=True)
        squares = jnp.transpose(jnp.broadcast_to(squares, (batch, 128)))[:16, :]
        squares_ref[...] = squares
        gained_ref[...] = jnp.transpose(value * gain_ref[...]).astype(BF16)
        for k in range(chips):
            out_ref[k, :own, :] = dot(w_ref[k], gained_ref[...]).astype(BF16)
            out_ref[k, own:, :] = squares.astype(BF16)

    return call(
        kernel,
        place,
        list(pieces) + [gain, weights],
        [
            shape((chips, own + 16, batch), BF16),
            shape((width, batch), BF16),
            shape((16, batch), F32),
        ],
        scratch=[pltpu.VMEM((batch, width), F32)],
        limit=8,
        name="project_first",
    )


def project_keep(place, weights, gained, squares, chips):
    own = weights.shape[1]
    batch = gained.shape[1]

    def kernel(place_ref, w_ref, gained_ref, squares_ref, out_ref):
        for k in range(chips):
            out_ref[k, :own, :] = dot(w_ref[chips + k], gained_ref[...]).astype(BF16)
            out_ref[k, own:, :] = squares_ref[...].astype(BF16)

    return call(
        kernel,
        place,
        [weights, gained, squares],
        [shape((chips, own + 16, batch), BF16)],
        name="project_keep",
    )[0]


def project_gate(place, weights, gained, conv_rows, x_cols, own, chips, earlier):
    width, batch = gained.shape
    count = 2 * chips

    def kernel(
        place_ref, w_ref, gained_ref, conv_ref, cols_ref, earlier_ref,
        give_ref, keep_ref, conv_to, cols_to, held, sems,
    ):
        pairs = owner_rows(w_ref, 1, place_ref, own, held, count)
        copies = fetch(pairs + [(conv_ref, conv_to), (cols_ref, cols_to)], sems)
        for out_ref, base in ((give_ref, 0), (keep_ref, chips)):
            for k in range(chips):
                copies[base + k].wait()
            for k in range(chips):
                out_ref[k] = dot(held[base + k], gained_ref[...]).astype(BF16)
        copies[count].wait()
        copies[count + 1].wait()

    return call(
        kernel,
        place,
        [in_hbm(weights), gained, in_hbm(conv_rows), in_hbm(x_cols), anywhere(earlier)],
        [shape((chips, own, batch), BF16)] * 2
        + [shape(conv_rows.shape, BF16), shape(x_cols.shape, BF16)],
        scratch=[
            pltpu.VMEM((count, own, width), BF16),
            pltpu.SemaphoreType.DMA((count + 2,)),
        ],
        limit=12,
        cost=count * own * width * 2,
        name="project_gate",
    )


def convolve(place, own_sum, received, conv_state, params, alive, x_cols, own, whole_width):
    taps, _, batch = conv_state.shape
    half = x_cols.shape[0] // 2
    count = len(received)

    def kernel(place_ref, own_ref, *refs):
        got = refs[:count]
        (
            state_ref,
            params_ref,
            alive_ref,
            cols_ref,
            new_ref,
            xa_ref,
            give_ref,
            keep_ref,
            scale_ref,
        ) = refs[count:]
        total = own_ref[...]
        for ref in got:
            total = total + ref[...].astype(F32)
        scale = lax.rsqrt(total[own : own + 8, :] / whole_width + 1e-05)
        scale_ref[...] = scale
        value = (total[:own] * scale[:1]).astype(BF16)
        held = alive_ref[:1, :] > 0
        mixed = params_ref[:, taps : taps + 1] * value.astype(F32)
        for k in range(taps):
            old = jnp.where(held, state_ref[k].astype(F32), 0.0)
            mixed = mixed + params_ref[:, k : k + 1] * old
            if k:
                new_ref[k - 1] = old.astype(BF16)
        new_ref[taps - 1] = value
        mixed = mixed + params_ref[:, taps + 1 : taps + 2]
        active = (mixed / (1.0 + jnp.exp(-mixed))).astype(BF16)
        xa_ref[...] = active
        core = place_ref[place_ref.shape[0] - 1]
        there = pl.multiple_of((1 - core) * half, half)
        here = pl.multiple_of(core * half, half)
        give_ref[...] = dot(cols_ref[pl.ds(there, half), :], active).astype(BF16)
        keep_ref[...] = dot(cols_ref[pl.ds(here, half), :], active)

    return call(
        kernel,
        place,
        [own_sum]
        + list(received)
        + [
            conv_state,
            params,
            alive,
            x_cols,
        ],
        [
            shape(conv_state.shape, BF16),
            shape((own, batch), BF16),
            shape((half, batch), BF16),
            shape((half, batch), F32),
            shape((8, batch), F32),
        ],
        limit=8,
        name="convolve",
    )


def ready_state(place, state, alive, earlier):
    own, nstate, batch = state.shape
    block = 128
    steps, lanes = own // block, batch // 128

    def kernel(place_ref, state_ref, alive_ref, earlier_ref, out_ref, held, wide, sems):
        copies = fetch(
            [(state_ref.at[pl.ds(i * block, block)], held.at[i]) for i in range(steps)], sems
        )
        for i in range(steps):
            copies[i].wait()
            old = held[i].reshape(block * nstate, batch).astype(F32)
            old = jnp.where(alive_ref[:1, :] > 0, old, 0.0)
            for c in range(lanes):
                wide[i % 2, c] = old[:, c * 128 : (c + 1) * 128]
                for n in range(nstate):
                    out_ref[n, i * block : (i + 1) * block, c * 128 : (c + 1) * 128] = wide[
                        i % 2, c, pl.ds(n, block, stride=nstate), :
                    ]

    return call(
        kernel,
        place,
        [in_hbm(state), alive, anywhere(earlier)],
        [shape((nstate, own, batch), F32)],
        scratch=[
            pltpu.VMEM((steps, block, nstate, batch), BF16),
            pltpu.VMEM((2, lanes, block * nstate, 128), F32),
            pltpu.SemaphoreType.DMA((steps,)),
        ],
        limit=16,
        cost=own * nstate * batch * 6,
        name="ready_state",
    )[0]


def scan(place, mine, other, dt_rows, params, state, xa, taps):
    nstate, own, batch = state.shape
    rank = dt_rows.shape[1]
    half = mine.shape[0]
    block = 128
    steps, lanes = own // block, batch // 128

    def kernel(place_ref, mine_ref, other_ref, dtw_ref, params_ref, state_ref, *refs):
        xa_ref, packed, value_ref, low, behind = refs
        core = place_ref[place_ref.shape[0] - 1]
        first = jnp.broadcast_to(core, mine_ref.shape) == 0
        low[:half] = jnp.where(first, mine_ref[...], other_ref[...])
        low[half:] = jnp.where(first, other_ref[...], mine_ref[...])
        for i in range(steps):
            here = slice(i * block, (i + 1) * block)
            pre = dot(dtw_ref[here, :], low[:rank, :]) + params_ref[here, taps + 2 : taps + 3]
            step = jnp.maximum(pre, 0.0) + jnp.log1p(jnp.exp(-jnp.abs(pre)))
            wide = xa_ref[here, :].astype(F32)
            drive = step * wide
            value = params_ref[here, taps + 3 : taps + 4] * wide
            for n in range(nstate):
                rate = params_ref[here, taps + 4 + n : taps + 5 + n]
                bm = low[rank + n : rank + n + 1, :].astype(F32)
                cm = low[rank + nstate + n : rank + nstate + n + 1, :].astype(F32)
                fresh = jnp.exp2(step * rate) * state_ref[n, here, :] + drive * bm
                for c in range(lanes):
                    behind[i % 2, c, pl.ds(n, block, stride=nstate), :] = fresh[
                        :, c * 128 : (c + 1) * 128
                    ]
                value = value + fresh * cm
            for c in range(lanes):
                packed[here, :, c * 128 : (c + 1) * 128] = (
                    behind[i % 2, c].reshape(block, nstate, 128).astype(BF16)
                )
            value_ref[here, :] = value

    pairs = [in_vmem(a) for a in (mine, other, dt_rows, params, state, xa)]
    return pl.pallas_call(
        kernel,
        grid_spec=pltpu.PrefetchScalarGridSpec(
            num_scalar_prefetch=1,
            grid=(),
            in_specs=[spec for _, spec in pairs],
            out_specs=[
                pl.BlockSpec(memory_space=pltpu.VMEM),
                pl.BlockSpec(memory_space=pltpu.VMEM),
            ],
            scratch_shapes=[
                pltpu.VMEM((2 * half, batch), BF16),
                pltpu.VMEM((2, lanes, block * nstate, 128), F32),
            ],
        ),
        out_shape=[
            pltpu.VMEM((own, nstate, batch), BF16),
            pltpu.VMEM((own, batch), F32),
        ],
        compiler_params=pltpu.CompilerParams(vmem_limit_bytes=18 * MIB),
        cost_estimate=pl.CostEstimate(flops=0, bytes_accessed=1, transcendentals=0),
        name="scan",
    )(place, *[array for array, _ in pairs])


def store_state(place, state, earlier):
    parts = 4
    rows = state.shape[0] // parts

    def kernel(place_ref, state_ref, earlier_ref, out_ref, sems):
        pairs = [
            (state_ref.at[i * rows : (i + 1) * rows], out_ref.at[i * rows : (i + 1) * rows])
            for i in range(parts)
        ]
        for copy in fetch(pairs, sems):
            copy.wait()

    pairs = [in_vmem(state), anywhere(earlier)]
    return pl.pallas_call(
        kernel,
        grid_spec=pltpu.PrefetchScalarGridSpec(
            num_scalar_prefetch=1,
            grid=(),
            in_specs=[spec for _, spec in pairs],
            out_specs=pl.BlockSpec(memory_space=pltpu.HBM),
            scratch_shapes=[pltpu.SemaphoreType.DMA((parts,))],
        ),
        out_shape=pltpu.HBM(state.shape, BF16),
        compiler_params=pltpu.CompilerParams(vmem_limit_bytes=4 * MIB),
        cost_estimate=pl.CostEstimate(
            flops=0, bytes_accessed=state.size * 2, transcendentals=0
        ),
        name="store_state",
    )(place, *[array for array, _ in pairs])


def gate_rows(place, value, zown, zgot, scale):
    own, batch = value.shape
    count = len(zgot)

    def kernel(place_ref, value_ref, zown_ref, *refs):
        scale_ref, gated_ref = refs[count:]
        total = zown_ref[...]
        for ref in refs[:count]:
            total = total + ref[...].astype(F32)
        gate = (total * scale_ref[:1, :]).astype(BF16).astype(F32)
        value = value_ref[...] * (gate / (1.0 + jnp.exp(-gate)))
        gated_ref[...] = jnp.transpose(value).astype(BF16)

    return call(
        kernel,
        place,
        [value, zown, *zgot, scale],
        [shape((batch, own), BF16)],
        name="gate_rows",
    )[0]


def mix_out(place, pieces, weights, parts, chips):
    batch, own = pieces[0].shape
    width = weights.shape[2]
    count = len(pieces)
    rows = batch // parts

    def kernel(place_ref, *refs):
        piece_refs = refs[:count]
        w_ref, own_ref = refs[count : count + 2]
        wire_refs = refs[count + 2 : -1]
        total = refs[-1]
        for j in range(count):
            term = dot(piece_refs[j][...], w_ref[j])
            total[...] = term if j == 0 else total[...] + term
        me = place_ref[2 * chips]
        for k in range(parts):
            start = pl.multiple_of((me ^ k) * rows, rows)
            value = total[pl.ds(start, rows), :]
            if k == 0:
                own_ref[...] = value
            else:
                wire_refs[k - 1][...] = value.astype(BF16)

    own_rows, *wires = call(
        kernel,
        place,
        list(pieces) + [weights],
        [shape((rows, width), F32)] + [shape((rows, width), BF16)] * (parts - 1),
        scratch=[pltpu.VMEM((batch, width), F32)],
        limit=8,
        name="mix_out",
    )
    return own_rows, wires


def held_by(assign_ref):
    batch = assign_ref.shape[1]
    requests = lax.broadcasted_iota(jnp.int32, (batch, batch), 0)
    return jnp.where(assign_ref[...] == requests, 1.0, 0.0).astype(BF16)


def query(place, pieces, assign, gain, weights, chips):
    rows, width = pieces[0].shape
    batch = rows * len(pieces)
    count = len(pieces)
    columns = weights.shape[1]
    steps = 5
    block = columns // steps
    half = batch // 2
    slots = half // chips

    def kernel(place_ref, *refs):
        piece_refs = refs[:count]
        assign_ref, gain_ref, w_ref, give_ref, keep_ref, stacked, ordered = refs[count:]
        me = place_ref[2 * chips]
        for k in range(count):
            start = pl.multiple_of((me ^ k) * rows, rows)
            stacked[pl.ds(start, rows), :] = piece_refs[k][...]
        chosen = held_by(assign_ref)
        stacked[...] = dot(chosen, stacked[...], ((0,), (0,))).astype(BF16)
        for k in range(2 * chips):
            start = pl.multiple_of(place_ref[k] * slots, slots)
            ordered[k * slots : (k + 1) * slots, :] = stacked[pl.ds(start, slots), :]
        value = ordered[...].astype(F32)
        squares = jnp.sum(value * value, axis=1, keepdims=True)
        squares = jnp.broadcast_to(squares, (batch, 128)).astype(BF16)
        give_ref[:, columns:] = squares[:half]
        keep_ref[:, columns:] = squares[half:]
        gained = (value * gain_ref[...]).astype(BF16)
        for j in range(steps):
            out = dot(gained, w_ref[:, j * block : (j + 1) * block]).astype(BF16)
            give_ref[:, j * block : (j + 1) * block] = out[:half]
            keep_ref[:, j * block : (j + 1) * block] = out[half:]

    return call(
        kernel,
        place,
        list(pieces) + [assign, gain, weights],
        [shape((half, columns + 128), BF16)] * 2,
        scratch=[pltpu.VMEM((batch, width), BF16)] * 2,
        limit=8,
        name="query",
    )


def head_out(place, pieces, assign, weights, parts, chips):
    slots, depth = pieces[0].shape
    count = len(pieces)
    batch = slots * count
    steps, block, width = weights.shape
    rows = batch // parts

    def kernel(place_ref, *refs):
        piece_refs = refs[:count]
        assign_ref, w_ref, own_ref = refs[count : count + 3]
        wire_refs = refs[count + 3 : -2]
        stacked, total = refs[-2:]
        mine = place_ref[2 * chips + 1]
        for j in range(count):
            start = pl.multiple_of((mine ^ j) * slots, slots)
            stacked[pl.ds(start, slots), :] = piece_refs[j][...]
        chosen = held_by(assign_ref)
        for j in range(steps):
            taken = dot(chosen, stacked[:, j * block : (j + 1) * block]).astype(BF16)
            term = dot(taken, w_ref[j])
            total[...] = term if j == 0 else total[...] + term
        me = place_ref[2 * chips]
        for k in range(parts):
            start = pl.multiple_of((me ^ k) * rows, rows)
            value = total[pl.ds(start, rows), :]
            if k == 0:
                own_ref[...] = value
            else:
                wire_refs[k - 1][...] = value.astype(BF16)

    own_rows, *wires = call(
        kernel,
        place,
        list(pieces) + [assign, weights],
        [shape((rows, width), F32)] + [shape((rows, width), BF16)] * (parts - 1),
        scratch=[pltpu.VMEM((batch, depth), BF16), pltpu.VMEM((batch, width), F32)],
        limit=8,
        name="head_out",
    )
    return own_rows, wires


def total_of(own, received):
    total = own
    for value in received:
        total = total + value.astype(F32)
    return total


def on_device(
    hidden_in,
    norm_gain_a,
    mixer_projection,
    conv_weight,
    conv_bias,
    conv_state,
    ssm_state,
    reset_ids,
    x_proj,
    dt_proj,
    dt_bias,
    a_log,
    d_skip,
    mixer_output,
    norm_gain_b,
    attention_projection,
    head_output,
    kv_cache,
    lengths,
    assign,
):
    batch = assign.shape[0]
    yz, gx = lax.axis_size("yz"), lax.axis_size("gx")
    chips = yz // 2
    me_yz, me_gx = lax.axis_index("yz"), lax.axis_index("gx")
    core = me_yz % 2
    width = hidden_in.shape[1]
    whole_width = width * yz
    own = mixer_projection.shape[1] // yz
    taps = conv_state.shape[1]

    owners = jnp.concatenate(
        [(me_yz ^ 1) ^ (2 * jnp.arange(chips)), me_yz ^ (2 * jnp.arange(chips))]
    ).astype(jnp.int32)
    place = jnp.concatenate([owners, jnp.stack([me_gx, me_yz, core]).astype(jnp.int32)])
    requests = jnp.arange(batch, dtype=jnp.int32)
    x_cols = jnp.transpose(x_proj)
    conv_rows = jnp.transpose(conv_state, (1, 0, 2))
    group_count, group_cols = attention_projection.shape[1:]
    slot_count = kv_cache.shape[0]

    got = swaps_gx([hidden_in] * (gx - 1), (0, 1, 2), (1, 2, 0))
    weights, hidden_here, gain = stage_first(
        place, mixer_projection, hidden_in, norm_gain_a[None, :], own, chips
    )
    got, weights = lax.optimization_barrier((got, weights))
    give, gained, squares = project_first(
        place, [hidden_here] + got, gain, weights, batch, chips
    )
    tall = chips * (own + 16)
    received = swap(give.reshape(tall, batch), "yz", 1)
    keep = project_keep(place, weights, gained, squares, chips)
    xown, wires = add_pairs(keep.reshape(tall, batch), received, chips, place, "add_x")
    xgot = swaps_chip(wires, (1, 2, 0), (2, 0, 0))
    give, keep, conv_rows, x_cols = project_gate(
        place, mixer_projection, gained, conv_rows, x_cols, own, chips, wires[0]
    )
    (conv_weight, a_log, reset_ids, dt_proj), wires = lax.optimization_barrier(
        ((conv_weight, a_log, reset_ids, dt_proj), wires)
    )
    alive = jnp.where(jnp.any(reset_ids[:, None] == requests[None, :], axis=0), 0.0, 1.0)
    alive = jnp.broadcast_to(alive[None, :].astype(F32), (8, batch))
    params = jnp.transpose(
        jnp.concatenate(
            [conv_weight, conv_bias[None], dt_bias[None], d_skip[None], -math.log2(math.e) * jnp.exp(a_log)], axis=0
        )
    )
    dt_rows = jnp.transpose(dt_proj)
    xgot, give, keep, conv_rows, x_cols, params, alive, dt_rows = lax.optimization_barrier(
        (xgot, give, keep, conv_rows, x_cols, params, alive, dt_rows)
    )
    z_received = swap(give.reshape(chips * own, batch), "yz", 1)
    conv_new, xa, give, part, scale = convolve(
        place, xown, xgot, conv_rows, params, alive, x_cols, own, whole_width
    )
    part, wire, z_odd, z_even = add_both(
        place, part, swap(give, "yz", 1), keep.reshape(chips * own, batch), z_received, chips
    )
    got = swaps_chip([wire] * (chips - 1), (0, 1, 2), (0, 1, 2))
    z_near = swap(z_odd, "yz", 2)
    old = ready_state(place, ssm_state, alive, part)
    got, old = lax.optimization_barrier((got, old))
    part = total_of(part, got)
    wire = part.astype(BF16)
    got = swaps_gx([wire] * (gx - 1), (0, 1, 2), (0, 0, 0))
    z_even = z_even + z_near.astype(F32)
    z_wires = [z_even[k * own : (k + 1) * own].astype(BF16) for k in range(1, chips // 2)]
    z_got = [swap(w, "yz", 4 * (k + 1)) for k, w in enumerate(z_wires)]
    part = total_of(part, got).astype(BF16)
    ssm_new, value = scan(
        place, part, swap(part, "yz", 1), dt_rows, params, old, xa, taps
    )
    gated = gate_rows(place, value, z_even[:own], z_got, scale)

    gated, attention_projection = lax.optimization_barrier((gated, attention_projection))
    flattened = attention_projection.reshape(width, group_count * group_cols)
    weights = stage_rows(place, mixer_output, yz, gated, True, chips, "stage_mix")
    got = swaps_chip([gated] * (chips - 1), (0, 1, 2), (0, 0, 0))
    ssm_new = store_state(place, ssm_new, gated)
    *got[1:], weights, flattened, ssm_new = lax.optimization_barrier(
        (*got[1:], weights, flattened, ssm_new)
    )
    pieces = gather_yz(gated, got)
    own_rows, wires = mix_out(place, pieces, weights, gx, chips)
    first_out = (hidden_in.astype(F32) + total_of(own_rows, swaps_gx(wires))).astype(BF16)

    pieces = [first_out] + swaps_gx([first_out] * (gx - 1))
    give, keep = query(place, pieces, assign[None, :], norm_gain_b[None, :], flattened, chips)
    entries, wires = add_pairs(keep, swap(give, "yz", 1), chips, place, "add_query")
    entries = total_of(entries, swaps_chip(wires, (1, 2, 0), (2, 0, 0)))
    scale = lax.rsqrt(entries[:, -1:] / whole_width + 1e-05)
    newest_entry = (entries[:, :-128] * scale).astype(BF16)
    newest_entry = newest_entry.reshape(slot_count, group_count, group_cols)
    head_dim = kv_cache.shape[3] // 2
    per_group = group_cols // head_dim - 2
    fresh_kv = newest_entry[:, :, per_group * head_dim :]
    query_vector = newest_entry[:, :, : per_group * head_dim].reshape(
        slot_count, group_count, per_group, head_dim
    )
    key_new = newest_entry[:, :, per_group * head_dim : (per_group + 1) * head_dim]
    value_new = newest_entry[:, :, (per_group + 1) * head_dim :]
    keys = kv_cache[..., :head_dim]
    values = kv_cache[..., head_dim:]
    factor = 1.0 / math.sqrt(head_dim)
    scores = (
        jnp.einsum("sghd,stgd->sght", query_vector, keys, preferred_element_type=F32) * factor
    )
    own_score = (
        jnp.einsum("sghd,sgd->sgh", query_vector, key_new, preferred_element_type=F32) * factor
    )
    positions = jnp.arange(kv_cache.shape[1], dtype=jnp.int32)
    valid = (positions[None, :] < lengths[:, None])[:, None, None, :]
    top = jnp.maximum(jnp.max(jnp.where(valid, scores, -1e30), axis=-1), own_score)
    expo = jnp.where(valid, jnp.exp(scores - top[..., None]), 0.0)
    expo_own = jnp.exp(own_score - top)
    total = jnp.sum(expo, axis=-1) + expo_own
    weights = (expo / total[..., None]).astype(BF16)
    weight_own = (expo_own / total).astype(BF16)
    attended = jnp.einsum("sght,stgd->sghd", weights, values, preferred_element_type=F32)
    attended = (
        attended + weight_own.astype(F32)[..., None] * value_new.astype(F32)[:, :, None, :]
    )
    heads = attended.astype(BF16).reshape(slot_count, group_count * per_group * head_dim)
    head_weights = stage_rows(place, head_output, 4, heads, False, chips, "stage_head")
    got = swaps_chip([heads] * (chips - 1), (0, 1, 2), (0, 0, 0))
    got[-1], head_weights = lax.optimization_barrier((got[-1], head_weights))
    pieces = gather_yz(heads, got)
    own_rows, wires = head_out(place, pieces, assign[None, :], head_weights, gx, chips)
    hidden_out = (first_out.astype(F32) + total_of(own_rows, swaps_gx(wires))).astype(BF16)
    return (hidden_out, ssm_new, jnp.transpose(conv_new, (1, 0, 2)), fresh_kv)


def solution(mesh):
    placed = (
        P(("groups", "gx"), "yz"),
        P("yz"),
        P(None, "gx", "yz"),
        P(None, ("gx", "yz")),
        P(("gx", "yz")),
        P(("gx", "yz"), None, "groups"),
        P(("gx", "yz"), None, "groups"),
        P("groups"),
        P(("gx", "yz"), None),
        P(None, ("gx", "yz")),
        P(("gx", "yz")),
        P(None, ("gx", "yz")),
        P(("gx", "yz")),
        P("gx", "yz"),
        P("yz"),
        P("yz", "gx", None),
        P("gx", "yz"),
        P(("groups", "yz"), None, "gx", None),
        P(("groups", "yz")),
        P("groups"),
    )
    return jax.shard_map(
        on_device,
        mesh=mesh,
        in_specs=placed,
        out_specs=(
            P(("groups", "gx"), "yz"),
            P(("gx", "yz"), None, "groups"),
            P(("gx", "yz"), None, "groups"),
            P(("groups", "yz"), "gx", None),
        ),
        check_vma=False,
    )
```

```python
import math

import jax
import jax.numpy as jnp
from jax import lax
from jax.experimental import pallas as pl
from jax.experimental.pallas import tpu as pltpu
from jax.sharding import PartitionSpec as P

F32 = jnp.float32
BF16 = jnp.bfloat16
MIB = 1 << 20


def swap(value, axis, bits):
    size = lax.axis_size(axis)
    return lax.ppermute(value, axis, [(i, i ^ bits) for i in range(size)])


def exchange(values, axis, step, order, depths):
    count = len(values)
    order = [k for k in order if k < count] + [k for k in range(count) if k not in order]
    got = {k: swap(values[k], axis, (k + 1) * step) for k in order}
    for k, depth in enumerate(depths[:count]):
        for _ in range(depth):
            got[k] = lax.optimization_barrier(got[k])
    return [got[k] for k in range(count)]


def swaps_gx(values, order=(2, 0, 1), depths=(1, 0, 2)):
    return exchange(values, "gx", 1, order, depths)


def swaps_chip(values, order=(2, 1, 0), depths=(0, 1, 2)):
    return exchange(values, "yz", 2, order, depths)


def gather_yz(value, got):
    mine = [value] + got
    other = [swap(v, "yz", 1) for v in mine]
    return [v for pair in zip(mine, other) for v in pair]


def dot(a, b, dims=((1,), (0,)), **kw):
    return lax.dot_general(a, b, (dims, ((), ())), preferred_element_type=F32, **kw)


def in_hbm(array):
    held = pltpu.with_memory_space_constraint(array, pltpu.HBM)
    return held, pl.BlockSpec(memory_space=pltpu.HBM)


def in_vmem(array):
    held = pltpu.with_memory_space_constraint(array, pltpu.VMEM)
    return held, pl.BlockSpec(memory_space=pltpu.VMEM)


def anywhere(array):
    return array, pl.BlockSpec(memory_space=pl.ANY)


def shape(dims, dtype):
    return pltpu.VMEM(tuple(dims), dtype)


def call(kernel, place, inputs, outs, scratch=(), limit=4, cost=None, name=None):
    pairs = [a if isinstance(a, tuple) else in_vmem(a) for a in inputs]
    return pl.pallas_call(
        kernel,
        grid_spec=pltpu.PrefetchScalarGridSpec(
            num_scalar_prefetch=1,
            grid=(),
            in_specs=[spec for _, spec in pairs],
            out_specs=[pl.BlockSpec(memory_space=pltpu.VMEM)] * len(outs),
            scratch_shapes=list(scratch),
        ),
        out_shape=outs,
        compiler_params=pltpu.CompilerParams(vmem_limit_bytes=limit * MIB),
        cost_estimate=cost and pl.CostEstimate(flops=0, bytes_accessed=cost, transcendentals=0),
        name=name,
    )(place, *[array for array, _ in pairs])


def fetch(pairs, sems):
    copies = [
        pltpu.make_async_copy(source, target, sems.at[k])
        for k, (source, target) in enumerate(pairs)
    ]
    for copy in copies:
        copy.start()
    return copies


def owner_rows(w_ref, half, place_ref, own, target, count):
    return [
        (
            w_ref.at[half, pl.ds(pl.multiple_of(place_ref[k] * own, own), own), :],
            target.at[k],
        )
        for k in range(count)
    ]


def stage_first(place, weights, hidden, gain, own, chips):
    width = weights.shape[2]

    def kernel(place_ref, w_ref, hidden_ref, gain_ref, held, hidden_to, gain_to, sems):
        pairs = owner_rows(w_ref, 0, place_ref, own, held, 2 * chips)
        for copy in fetch(pairs + [(hidden_ref, hidden_to), (gain_ref, gain_to)], sems):
            copy.wait()

    return call(
        kernel,
        place,
        [in_hbm(weights), in_hbm(hidden), in_hbm(gain)],
        [
            shape((2 * chips, own, width), BF16),
            shape(hidden.shape, BF16),
            shape(gain.shape, F32),
        ],
        scratch=[pltpu.SemaphoreType.DMA((2 * chips + 2,))],
        limit=4,
        cost=2 * chips * own * width * 2,
        name="stage_first",
    )


def stage_rows(place, weights, count, earlier, ordered, chips, name):
    rows, width = weights.shape
    block = rows // count

    def kernel(place_ref, w_ref, earlier_ref, held, sems):
        pairs = []
        for k in range(count):
            at = place_ref[2 * chips + 1] ^ k if ordered else k
            pairs.append(
                (w_ref.at[pl.ds(pl.multiple_of(at * block, block), block), :], held.at[k])
            )
        for copy in fetch(pairs, sems):
            copy.wait()

    return call(
        kernel,
        place,
        [in_hbm(weights), anywhere(earlier)],
        [shape((count, block, width), BF16)],
        scratch=[pltpu.SemaphoreType.DMA((count,))],
        limit=4,
        cost=rows * width * 2,
        name=name,
    )[0]


def add_pairs(keep, received, parts, place, name):
    rows = keep.shape[0] // parts
    width = keep.shape[1]

    def kernel(place_ref, keep_ref, received_ref, own_ref, *wire_refs):
        for k in range(parts):
            block = pl.ds(k * rows, rows)
            total = keep_ref[block, :].astype(F32) + received_ref[block, :].astype(F32)
            if k == 0:
                own_ref[...] = total
            else:
                wire_refs[k - 1][...] = total.astype(BF16)

    own, *wires = call(
        kernel,
        place,
        [keep, received],
        [shape((rows, width), F32)] + [shape((rows, width), BF16)] * (parts - 1),
        name=name,
    )
    return own, wires


def add_both(place, part, received, keep, z_received, parts):
    half, batch = part.shape
    own = keep.shape[0] // parts
    even = parts // 2 * own

    def kernel(place_ref, part_ref, received_ref, keep_ref, z_ref, sum_ref, wire_ref, odd_ref, z_to):
        total = part_ref[...] + received_ref[...].astype(F32)
        sum_ref[...] = total
        wire_ref[...] = total.astype(BF16)
        for k in range(parts):
            block = pl.ds(k * own, own)
            z = keep_ref[block, :].astype(F32) + z_ref[block, :].astype(F32)
            start = k // 2 * own
            if k % 2:
                odd_ref[start : start + own, :] = z.astype(BF16)
            else:
                z_to[start : start + own, :] = z

    return call(
        kernel,
        place,
        [part, received, keep, z_received],
        [
            shape((half, batch), F32),
            shape((half, batch), BF16),
            shape((even, batch), BF16),
            shape((even, batch), F32),
        ],
        name="add_both",
    )


def project_first(place, pieces, gain, weights, batch, chips):
    own, width = weights.shape[1:]
    rows = pieces[0].shape[0]
    count = len(pieces)

    def kernel(place_ref, *refs):
        piece_refs = refs[:count]
        gain_ref, w_ref, out_ref, gained_ref, squares_ref, wide = refs[count:]
        me = place_ref[2 * chips]
        for k in range(count):
            start = pl.multiple_of((me ^ k) * rows, rows)
            wide[pl.ds(start, rows), :] = piece_refs[k][...].astype(F32)
        value = wide[...]
        squares = jnp.sum(value * value, axis=1, keepdims=True)
        squares = jnp.transpose(jnp.broadcast_to(squares, (batch, 128)))[:16, :]
        squares_ref[...] = squares
        gained_ref[...] = jnp.transpose(value * gain_ref[...]).astype(BF16)
        for k in range(chips):
            out_ref[k, :own, :] = dot(w_ref[k], gained_ref[...]).astype(BF16)
            out_ref[k, own:, :] = squares.astype(BF16)

    return call(
        kernel,
        place,
        list(pieces) + [gain, weights],
        [
            shape((chips, own + 16, batch), BF16),
            shape((width, batch), BF16),
            shape((16, batch), F32),
        ],
        scratch=[pltpu.VMEM((batch, width), F32)],
        limit=8,
        name="project_first",
    )


def project_keep(place, weights, gained, squares, chips):
    own = weights.shape[1]
    batch = gained.shape[1]

    def kernel(place_ref, w_ref, gained_ref, squares_ref, out_ref):
        for k in range(chips):
            out_ref[k, :own, :] = dot(w_ref[chips + k], gained_ref[...]).astype(BF16)
            out_ref[k, own:, :] = squares_ref[...].astype(BF16)

    return call(
        kernel,
        place,
        [weights, gained, squares],
        [shape((chips, own + 16, batch), BF16)],
        name="project_keep",
    )[0]


def project_gate(place, weights, gained, conv_rows, x_cols, own, chips, earlier):
    width, batch = gained.shape
    count = 2 * chips

    def kernel(
        place_ref, w_ref, gained_ref, conv_ref, cols_ref, earlier_ref,
        give_ref, keep_ref, conv_to, cols_to, held, sems,
    ):
        pairs = owner_rows(w_ref, 1, place_ref, own, held, count)
        copies = fetch(pairs + [(conv_ref, conv_to), (cols_ref, cols_to)], sems)
        for out_ref, base in ((give_ref, 0), (keep_ref, chips)):
            for k in range(chips):
                copies[base + k].wait()
            for k in range(chips):
                out_ref[k] = dot(held[base + k], gained_ref[...]).astype(BF16)
        copies[count].wait()
        copies[count + 1].wait()

    return call(
        kernel,
        place,
        [in_hbm(weights), gained, in_hbm(conv_rows), in_hbm(x_cols), anywhere(earlier)],
        [shape((chips, own, batch), BF16)] * 2
        + [shape(conv_rows.shape, BF16), shape(x_cols.shape, BF16)],
        scratch=[
            pltpu.VMEM((count, own, width), BF16),
            pltpu.SemaphoreType.DMA((count + 2,)),
        ],
        limit=12,
        cost=count * own * width * 2,
        name="project_gate",
    )


def convolve(place, own_sum, received, conv_state, params, alive, x_cols, own, whole_width):
    taps, _, batch = conv_state.shape
    half = x_cols.shape[0] // 2
    count = len(received)

    def kernel(place_ref, own_ref, *refs):
        got = refs[:count]
        (
            state_ref,
            params_ref,
            alive_ref,
            cols_ref,
            new_ref,
            xa_ref,
            give_ref,
            keep_ref,
            scale_ref,
        ) = refs[count:]
        total = own_ref[...]
        for ref in got:
            total = total + ref[...].astype(F32)
        scale = lax.rsqrt(total[own : own + 8, :] / whole_width + 1e-05)
        scale_ref[...] = scale
        value = (total[:own] * scale[:1]).astype(BF16)
        held = alive_ref[:1, :] > 0
        mixed = params_ref[:, taps : taps + 1] * value.astype(F32)
        for k in range(taps):
            old = jnp.where(held, state_ref[k].astype(F32), 0.0)
            mixed = mixed + params_ref[:, k : k + 1] * old
            if k:
                new_ref[k - 1] = old.astype(BF16)
        new_ref[taps - 1] = value
        mixed = mixed + params_ref[:, taps + 1 : taps + 2]
        active = (mixed / (1.0 + jnp.exp(-mixed))).astype(BF16)
        xa_ref[...] = active
        core = place_ref[place_ref.shape[0] - 1]
        there = pl.multiple_of((1 - core) * half, half)
        here = pl.multiple_of(core * half, half)
        give_ref[...] = dot(cols_ref[pl.ds(there, half), :], active).astype(BF16)
        keep_ref[...] = dot(cols_ref[pl.ds(here, half), :], active)

    return call(
        kernel,
        place,
        [own_sum]
        + list(received)
        + [
            conv_state,
            params,
            alive,
            x_cols,
        ],
        [
            shape(conv_state.shape, BF16),
            shape((own, batch), BF16),
            shape((half, batch), BF16),
            shape((half, batch), F32),
            shape((8, batch), F32),
        ],
        limit=8,
        name="convolve",
    )


def ready_state(place, state, alive, earlier):
    own, nstate, batch = state.shape
    block = 128
    steps, lanes = own // block, batch // 128

    def kernel(place_ref, state_ref, alive_ref, earlier_ref, out_ref, held, wide, sems):
        copies = fetch(
            [(state_ref.at[pl.ds(i * block, block)], held.at[i]) for i in range(steps)], sems
        )
        for i in range(steps):
            copies[i].wait()
            old = held[i].reshape(block * nstate, batch).astype(F32)
            old = jnp.where(alive_ref[:1, :] > 0, old, 0.0)
            for c in range(lanes):
                wide[i % 2, c] = old[:, c * 128 : (c + 1) * 128]
                for n in range(nstate):
                    out_ref[n, i * block : (i + 1) * block, c * 128 : (c + 1) * 128] = wide[
                        i % 2, c, pl.ds(n, block, stride=nstate), :
                    ]

    return call(
        kernel,
        place,
        [in_hbm(state), alive, anywhere(earlier)],
        [shape((nstate, own, batch), F32)],
        scratch=[
            pltpu.VMEM((steps, block, nstate, batch), BF16),
            pltpu.VMEM((2, lanes, block * nstate, 128), F32),
            pltpu.SemaphoreType.DMA((steps,)),
        ],
        limit=16,
        cost=own * nstate * batch * 6,
        name="ready_state",
    )[0]


def scan(place, mine, other, dt_rows, params, state, xa, taps):
    nstate, own, batch = state.shape
    rank = dt_rows.shape[1]
    half = mine.shape[0]
    block = 128
    steps, lanes = own // block, batch // 128

    def kernel(place_ref, mine_ref, other_ref, dtw_ref, params_ref, state_ref, *refs):
        xa_ref, packed, value_ref, low, behind = refs
        core = place_ref[place_ref.shape[0] - 1]
        first = jnp.broadcast_to(core, mine_ref.shape) == 0
        low[:half] = jnp.where(first, mine_ref[...], other_ref[...])
        low[half:] = jnp.where(first, other_ref[...], mine_ref[...])
        for i in range(steps):
            here = slice(i * block, (i + 1) * block)
            pre = dot(dtw_ref[here, :], low[:rank, :]) + params_ref[here, taps + 2 : taps + 3]
            step = jnp.maximum(pre, 0.0) + jnp.log1p(jnp.exp(-jnp.abs(pre)))
            wide = xa_ref[here, :].astype(F32)
            drive = step * wide
            value = params_ref[here, taps + 3 : taps + 4] * wide
            for n in range(nstate):
                rate = params_ref[here, taps + 4 + n : taps + 5 + n]
                bm = low[rank + n : rank + n + 1, :].astype(F32)
                cm = low[rank + nstate + n : rank + nstate + n + 1, :].astype(F32)
                fresh = jnp.exp2(step * rate) * state_ref[n, here, :] + drive * bm
                for c in range(lanes):
                    behind[i % 2, c, pl.ds(n, block, stride=nstate), :] = fresh[
                        :, c * 128 : (c + 1) * 128
                    ]
                value = value + fresh * cm
            for c in range(lanes):
                packed[here, :, c * 128 : (c + 1) * 128] = (
                    behind[i % 2, c].reshape(block, nstate, 128).astype(BF16)
                )
            value_ref[here, :] = value

    pairs = [in_vmem(a) for a in (mine, other, dt_rows, params, state, xa)]
    return pl.pallas_call(
        kernel,
        grid_spec=pltpu.PrefetchScalarGridSpec(
            num_scalar_prefetch=1,
            grid=(),
            in_specs=[spec for _, spec in pairs],
            out_specs=[
                pl.BlockSpec(memory_space=pltpu.VMEM),
                pl.BlockSpec(memory_space=pltpu.VMEM),
            ],
            scratch_shapes=[
                pltpu.VMEM((2 * half, batch), BF16),
                pltpu.VMEM((2, lanes, block * nstate, 128), F32),
            ],
        ),
        out_shape=[
            pltpu.VMEM((own, nstate, batch), BF16),
            pltpu.VMEM((own, batch), F32),
        ],
        compiler_params=pltpu.CompilerParams(vmem_limit_bytes=18 * MIB),
        cost_estimate=pl.CostEstimate(flops=0, bytes_accessed=1, transcendentals=0),
        name="scan",
    )(place, *[array for array, _ in pairs])


def store_state(place, state, earlier):
    parts = 4
    rows = state.shape[0] // parts

    def kernel(place_ref, state_ref, earlier_ref, out_ref, sems):
        pairs = [
            (state_ref.at[i * rows : (i + 1) * rows], out_ref.at[i * rows : (i + 1) * rows])
            for i in range(parts)
        ]
        for copy in fetch(pairs, sems):
            copy.wait()

    pairs = [in_vmem(state), anywhere(earlier)]
    return pl.pallas_call(
        kernel,
        grid_spec=pltpu.PrefetchScalarGridSpec(
            num_scalar_prefetch=1,
            grid=(),
            in_specs=[spec for _, spec in pairs],
            out_specs=pl.BlockSpec(memory_space=pltpu.HBM),
            scratch_shapes=[pltpu.SemaphoreType.DMA((parts,))],
        ),
        out_shape=pltpu.HBM(state.shape, BF16),
        compiler_params=pltpu.CompilerParams(vmem_limit_bytes=4 * MIB),
        cost_estimate=pl.CostEstimate(
            flops=0, bytes_accessed=state.size * 2, transcendentals=0
        ),
        name="store_state",
    )(place, *[array for array, _ in pairs])


def gate_rows(place, value, zown, zgot, scale):
    own, batch = value.shape
    count = len(zgot)

    def kernel(place_ref, value_ref, zown_ref, *refs):
        scale_ref, gated_ref = refs[count:]
        total = zown_ref[...]
        for ref in refs[:count]:
            total = total + ref[...].astype(F32)
        gate = (total * scale_ref[:1, :]).astype(BF16).astype(F32)
        value = value_ref[...] * (gate / (1.0 + jnp.exp(-gate)))
        gated_ref[...] = jnp.transpose(value).astype(BF16)

    return call(
        kernel,
        place,
        [value, zown, *zgot, scale],
        [shape((batch, own), BF16)],
        name="gate_rows",
    )[0]


def mix_out(place, pieces, weights, parts, chips):
    batch, own = pieces[0].shape
    width = weights.shape[2]
    count = len(pieces)
    rows = batch // parts

    def kernel(place_ref, *refs):
        piece_refs = refs[:count]
        w_ref, own_ref = refs[count : count + 2]
        wire_refs = refs[count + 2 : -1]
        total = refs[-1]
        value = dot(piece_refs[0][...], w_ref[0])
        for j in range(1, count):
            value = value + dot(piece_refs[j][...], w_ref[j])
        total[...] = value
        me = place_ref[2 * chips]
        for k in range(parts):
            start = pl.multiple_of((me ^ k) * rows, rows)
            value = total[pl.ds(start, rows), :]
            if k == 0:
                own_ref[...] = value
            else:
                wire_refs[k - 1][...] = value.astype(BF16)

    own_rows, *wires = call(
        kernel,
        place,
        list(pieces) + [weights],
        [shape((rows, width), F32)] + [shape((rows, width), BF16)] * (parts - 1),
        scratch=[pltpu.VMEM((batch, width), F32)],
        limit=8,
        name="mix_out",
    )
    return own_rows, wires


def held_by(assign_ref):
    batch = assign_ref.shape[1]
    requests = lax.broadcasted_iota(jnp.int32, (batch, batch), 0)
    return jnp.where(assign_ref[...] == requests, 1.0, 0.0).astype(BF16)


def query(place, pieces, assign, gain, weights, chips):
    rows, width = pieces[0].shape
    batch = rows * len(pieces)
    count = len(pieces)
    columns = weights.shape[1]
    steps = 5
    block = columns // steps
    half = batch // 2
    slots = half // chips

    def kernel(place_ref, *refs):
        piece_refs = refs[:count]
        assign_ref, gain_ref, w_ref, give_ref, keep_ref, stacked, ordered = refs[count:]
        me = place_ref[2 * chips]
        for k in range(count):
            start = pl.multiple_of((me ^ k) * rows, rows)
            stacked[pl.ds(start, rows), :] = piece_refs[k][...]
        chosen = held_by(assign_ref)
        stacked[...] = dot(chosen, stacked[...], ((0,), (0,))).astype(BF16)
        for k in range(2 * chips):
            start = pl.multiple_of(place_ref[k] * slots, slots)
            ordered[k * slots : (k + 1) * slots, :] = stacked[pl.ds(start, slots), :]
        value = ordered[...].astype(F32)
        squares = jnp.sum(value * value, axis=1, keepdims=True)
        squares = jnp.broadcast_to(squares, (batch, 128)).astype(BF16)
        give_ref[:, columns:] = squares[:half]
        keep_ref[:, columns:] = squares[half:]
        gained = (value * gain_ref[...]).astype(BF16)
        out = dot(gained, w_ref[...]).astype(BF16)
        give_ref[:, :columns] = out[:half]
        keep_ref[:, :columns] = out[half:]

    return call(
        kernel,
        place,
        list(pieces) + [assign, gain, weights],
        [shape((half, columns + 128), BF16)] * 2,
        scratch=[pltpu.VMEM((batch, width), BF16)] * 2,
        limit=8,
        name="query",
    )


def head_out(place, pieces, assign, weights, parts, chips):
    slots, depth = pieces[0].shape
    count = len(pieces)
    batch = slots * count
    steps, block, width = weights.shape
    rows = batch // parts

    def kernel(place_ref, *refs):
        piece_refs = refs[:count]
        assign_ref, w_ref, own_ref = refs[count : count + 3]
        wire_refs = refs[count + 3 : -2]
        stacked, total = refs[-2:]
        mine = place_ref[2 * chips + 1]
        for j in range(count):
            start = pl.multiple_of((mine ^ j) * slots, slots)
            stacked[pl.ds(start, slots), :] = piece_refs[j][...]
        chosen = held_by(assign_ref)
        taken = dot(chosen, stacked[...]).astype(BF16)
        value = dot(taken[:, :block], w_ref[0])
        for j in range(1, steps):
            value = value + dot(taken[:, j * block : (j + 1) * block], w_ref[j])
        total[...] = value
        me = place_ref[2 * chips]
        for k in range(parts):
            start = pl.multiple_of((me ^ k) * rows, rows)
            value = total[pl.ds(start, rows), :]
            if k == 0:
                own_ref[...] = value
            else:
                wire_refs[k - 1][...] = value.astype(BF16)

    own_rows, *wires = call(
        kernel,
        place,
        list(pieces) + [assign, weights],
        [shape((rows, width), F32)] + [shape((rows, width), BF16)] * (parts - 1),
        scratch=[pltpu.VMEM((batch, depth), BF16), pltpu.VMEM((batch, width), F32)],
        limit=8,
        name="head_out",
    )
    return own_rows, wires


def total_of(own, received):
    total = own
    for value in received:
        total = total + value.astype(F32)
    return total


def on_device(
    hidden_in,
    norm_gain_a,
    mixer_projection,
    conv_weight,
    conv_bias,
    conv_state,
    ssm_state,
    reset_ids,
    x_proj,
    dt_proj,
    dt_bias,
    a_log,
    d_skip,
    mixer_output,
    norm_gain_b,
    attention_projection,
    head_output,
    kv_cache,
    lengths,
    assign,
):
    batch = assign.shape[0]
    yz, gx = lax.axis_size("yz"), lax.axis_size("gx")
    chips = yz // 2
    me_yz, me_gx = lax.axis_index("yz"), lax.axis_index("gx")
    core = me_yz % 2
    width = hidden_in.shape[1]
    whole_width = width * yz
    own = mixer_projection.shape[1] // yz
    taps = conv_state.shape[1]

    owners = jnp.concatenate(
        [(me_yz ^ 1) ^ (2 * jnp.arange(chips)), me_yz ^ (2 * jnp.arange(chips))]
    ).astype(jnp.int32)
    place = jnp.concatenate([owners, jnp.stack([me_gx, me_yz, core]).astype(jnp.int32)])
    requests = jnp.arange(batch, dtype=jnp.int32)
    x_cols = jnp.transpose(x_proj)
    conv_rows = jnp.transpose(conv_state, (1, 0, 2))
    group_count, group_cols = attention_projection.shape[1:]
    slot_count = kv_cache.shape[0]

    got = swaps_gx([hidden_in] * (gx - 1), (0, 1, 2), (1, 2, 0))
    weights, hidden_here, gain = stage_first(
        place, mixer_projection, hidden_in, norm_gain_a[None, :], own, chips
    )
    got, weights = lax.optimization_barrier((got, weights))
    give, gained, squares = project_first(
        place, [hidden_here] + got, gain, weights, batch, chips
    )
    tall = chips * (own + 16)
    received = swap(give.reshape(tall, batch), "yz", 1)
    keep = project_keep(place, weights, gained, squares, chips)
    xown, wires = add_pairs(keep.reshape(tall, batch), received, chips, place, "add_x")
    xgot = swaps_chip(wires, (1, 2, 0), (2, 0, 0))
    give, keep, conv_rows, x_cols = project_gate(
        place, mixer_projection, gained, conv_rows, x_cols, own, chips, wires[0]
    )
    (conv_weight, a_log, reset_ids, dt_proj), wires = lax.optimization_barrier(
        ((conv_weight, a_log, reset_ids, dt_proj), wires)
    )
    alive = jnp.where(jnp.any(reset_ids[:, None] == requests[None, :], axis=0), 0.0, 1.0)
    alive = jnp.broadcast_to(alive[None, :].astype(F32), (8, batch))
    params = jnp.transpose(
        jnp.concatenate(
            [conv_weight, conv_bias[None], dt_bias[None], d_skip[None], -math.log2(math.e) * jnp.exp(a_log)], axis=0
        )
    )
    dt_rows = jnp.transpose(dt_proj)
    xgot, give, keep, conv_rows, x_cols, params, alive, dt_rows = lax.optimization_barrier(
        (xgot, give, keep, conv_rows, x_cols, params, alive, dt_rows)
    )
    z_received = swap(give.reshape(chips * own, batch), "yz", 1)
    conv_new, xa, give, part, scale = convolve(
        place, xown, xgot, conv_rows, params, alive, x_cols, own, whole_width
    )
    part, wire, z_odd, z_even = add_both(
        place, part, swap(give, "yz", 1), keep.reshape(chips * own, batch), z_received, chips
    )
    got = swaps_chip([wire] * (chips - 1), (0, 1, 2), (0, 1, 2))
    z_near = swap(z_odd, "yz", 2)
    old = ready_state(place, ssm_state, alive, part)
    got, old = lax.optimization_barrier((got, old))
    part = total_of(part, got)
    wire = part.astype(BF16)
    got = swaps_gx([wire] * (gx - 1), (0, 1, 2), (0, 0, 0))
    z_even = z_even + z_near.astype(F32)
    z_wires = [z_even[k * own : (k + 1) * own].astype(BF16) for k in range(1, chips // 2)]
    z_got = [swap(w, "yz", 4 * (k + 1)) for k, w in enumerate(z_wires)]
    part = total_of(part, got).astype(BF16)
    ssm_new, value = scan(
        place, part, swap(part, "yz", 1), dt_rows, params, old, xa, taps
    )
    gated = gate_rows(place, value, z_even[:own], z_got, scale)

    gated, attention_projection = lax.optimization_barrier((gated, attention_projection))
    flattened = attention_projection.reshape(width, group_count * group_cols)
    weights = stage_rows(place, mixer_output, yz, gated, True, chips, "stage_mix")
    got = swaps_chip([gated] * (chips - 1), (0, 1, 2), (0, 0, 0))
    ssm_new = store_state(place, ssm_new, gated)
    *got[1:], weights, flattened, ssm_new = lax.optimization_barrier(
        (*got[1:], weights, flattened, ssm_new)
    )
    pieces = gather_yz(gated, got)
    own_rows, wires = mix_out(place, pieces, weights, gx, chips)
    first_out = (hidden_in.astype(F32) + total_of(own_rows, swaps_gx(wires))).astype(BF16)

    pieces = [first_out] + swaps_gx([first_out] * (gx - 1))
    give, keep = query(place, pieces, assign[None, :], norm_gain_b[None, :], flattened, chips)
    entries, wires = add_pairs(keep, swap(give, "yz", 1), chips, place, "add_query")
    entries = total_of(entries, swaps_chip(wires, (1, 2, 0), (2, 0, 0)))
    scale = lax.rsqrt(entries[:, -1:] / whole_width + 1e-05)
    newest_entry = (entries[:, :-128] * scale).astype(BF16)
    newest_entry = newest_entry.reshape(slot_count, group_count, group_cols)
    head_dim = kv_cache.shape[3] // 2
    per_group = group_cols // head_dim - 2
    fresh_kv = newest_entry[:, :, per_group * head_dim :]
    query_vector = newest_entry[:, :, : per_group * head_dim].reshape(
        slot_count, group_count, per_group, head_dim
    )
    key_new = newest_entry[:, :, per_group * head_dim : (per_group + 1) * head_dim]
    value_new = newest_entry[:, :, (per_group + 1) * head_dim :]
    keys = kv_cache[..., :head_dim]
    values = kv_cache[..., head_dim:]
    factor = 1.0 / math.sqrt(head_dim)
    scores = (
        jnp.einsum("sghd,stgd->sght", query_vector, keys, preferred_element_type=F32) * factor
    )
    own_score = (
        jnp.einsum("sghd,sgd->sgh", query_vector, key_new, preferred_element_type=F32) * factor
    )
    positions = jnp.arange(kv_cache.shape[1], dtype=jnp.int32)
    valid = (positions[None, :] < lengths[:, None])[:, None, None, :]
    top = jnp.maximum(jnp.max(jnp.where(valid, scores, -1e30), axis=-1), own_score)
    expo = jnp.where(valid, jnp.exp(scores - top[..., None]), 0.0)
    expo_own = jnp.exp(own_score - top)
    total = jnp.sum(expo, axis=-1) + expo_own
    weights = (expo / total[..., None]).astype(BF16)
    weight_own = (expo_own / total).astype(BF16)
    attended = jnp.einsum("sght,stgd->sghd", weights, values, preferred_element_type=F32)
    attended = (
        attended + weight_own.astype(F32)[..., None] * value_new.astype(F32)[:, :, None, :]
    )
    heads = attended.astype(BF16).reshape(slot_count, group_count * per_group * head_dim)
    head_weights = stage_rows(place, head_output, 4, heads, False, chips, "stage_head")
    got = swaps_chip([heads] * (chips - 1), (0, 1, 2), (0, 0, 0))
    got[-1], head_weights = lax.optimization_barrier((got[-1], head_weights))
    pieces = gather_yz(heads, got)
    own_rows, wires = head_out(place, pieces, assign[None, :], head_weights, gx, chips)
    hidden_out = (first_out.astype(F32) + total_of(own_rows, swaps_gx(wires))).astype(BF16)
    return (hidden_out, ssm_new, jnp.transpose(conv_new, (1, 0, 2)), fresh_kv)


def solution(mesh):
    placed = (
        P(("groups", "gx"), "yz"),
        P("yz"),
        P(None, "gx", "yz"),
        P(None, ("gx", "yz")),
        P(("gx", "yz")),
        P(("gx", "yz"), None, "groups"),
        P(("gx", "yz"), None, "groups"),
        P("groups"),
        P(("gx", "yz"), None),
        P(None, ("gx", "yz")),
        P(("gx", "yz")),
        P(None, ("gx", "yz")),
        P(("gx", "yz")),
        P("gx", "yz"),
        P("yz"),
        P("yz", "gx", None),
        P("gx", "yz"),
        P(("groups", "yz"), None, "gx", None),
        P(("groups", "yz")),
        P("groups"),
    )
    return jax.shard_map(
        on_device,
        mesh=mesh,
        in_specs=placed,
        out_specs=(
            P(("groups", "gx"), "yz"),
            P(("gx", "yz"), None, "groups"),
            P(("gx", "yz"), None, "groups"),
            P(("groups", "yz"), "gx", None),
        ),
        check_vma=False,
    )
```
